256 devices in a mesh: req: 32 (over z, x), tp: 8 (over y, core).
Axes of the slice: x: 4, y: 4, z: 8, core: 2. Of those that a mesh axis runs over, the one named last changes fastest.
Arguments:
- queries: bfloat16 [2048, 7168], P('req', 'tp'), may hold values from -8 to 8
- resident_kv: bfloat16 [6144, 64, 2048], P('req', None, 'tp'), may hold values from -8 to 8
- swap_kv: bfloat16 [1024, 64, 2048], P('req', None, 'tp'), may hold values from -8 to 8
- page_table: int32 [2048, 4], P('req'), may hold values from 0 to 255, as said below
- lengths: int32 [2048], P('req'), may hold values from 65 to 256, as said below
- resume_source: int32 [2048, 1], replicated, may hold values from 0 to 31; in each aligned block of 64 rows (0 to 63, 64 to 127, ...) at most 4 rows name the same one
- resume_page: int32 [2048], replicated, may hold values from 0 to 31
- seg_lengths: int32 [32, 32], P('req'), may hold values from 1 to 4, 64 in all within a row
- segment_adapter_holder: int32 [1024, 1], replicated, may hold values from 0 to 31; in each aligned block of 32 rows (0 to 31, 32 to 63, ...) at most 2 rows name the same one
- seg_slot: int32 [1024], replicated, may hold values from 0 to 15
- adapter_down: bfloat16 [512, 64, 7168], P('req', None, 'tp'), may hold values from -0.0625 to 0.0625
- adapter_up: bfloat16 [512, 64, 7168], P('req', None, 'tp'), may hold values from -0.75 to 0.75
Outputs:
- attention: bfloat16 [2048, 7168], P('req', 'tp')
- adapter_delta: bfloat16 [2048, 7168], P('req', 'tp')
- arrived_pages: bfloat16 [2048, 64, 2048], P('req', None, 'tp')
The draws below stay inside these ranges and needn't reach their ends.
Inputs may be any that keep to these rules, and one draw needn't show every extreme that they name: `page_table`: within each block of 64 rows every number of 0 to 255 stands exactly once; numbers under 192 name the block's resident pages, 192 + j names the block's j-th resumed page. `lengths`: some request holds exactly 256 tokens. `resume_source`: rows come in blocks of 64, one block for each index of req in order; within one block no value stands more than 4 times. `seg_lengths`: each row sums to 64. `segment_adapter_holder`: rows come in blocks of 32, one block for each index of req in order; within one block no value stands more than 2 times.
All inputs are finite; a program needn't handle non-finite values.
Results may differ from the reference program's by a relative error of at most 0.011.
Values may be sent and summed in bfloat16 or wider, within the bound.
A program may use at most 128 MiB of HBM per device.

```python
import math
import jax
import jax.numpy as jnp
import numpy as np
from jax import lax

D = 7168
QH = 56
KVH = 8
HD = 128
R = 64
PAGE = 64
SEGMAX = 4
REQ_DEV = 64
MAXP = 4
ADP_DEV = 16
SEGS = 32
RES_ROWS = 64
POOL = 192
SWAP_PAGES = 32
CAPA = 2
CAPK = 4
REQS = 2048
SEG_ALL = 1024
RESUMED = 2048
RESIDENT = 6144
SWAPPED = 1024
ADAPTERS = 512
N_REQ = 32


def shuffled(key):
    return jax.random.permutation(key, REQ_DEV * MAXP)


def draw_queries(key, part):
    key = jax.random.fold_in(key, 3)
    key_base = jax.random.fold_in(key, 0)
    result = jnp.clip(1.5 * jax.random.normal(key_base, (REQS, QH, HD), jnp.float32), -6.0, 6.0)
    return result.reshape(REQS, QH * HD).astype(jnp.bfloat16)


def draw_resident_kv(key, part):
    key = jax.random.fold_in(key, 5)
    key_base = jax.random.fold_in(key, 0)
    cache = jnp.clip(jax.random.normal(key_base, (RESIDENT, PAGE, KVH, 2, HD), jnp.float32), -6.0, 6.0)
    return cache.reshape(RESIDENT, PAGE, KVH * 2 * HD).astype(jnp.bfloat16)


def draw_swap_kv(key, part):
    key = jax.random.fold_in(key, 7)
    key_base = jax.random.fold_in(key, 0)
    cache = jnp.clip(jax.random.normal(key_base, (SWAPPED, PAGE, KVH, 2, HD), jnp.float32), -6.0, 6.0)
    return cache.reshape(SWAPPED, PAGE, KVH * 2 * HD).astype(jnp.bfloat16)


def draw_page_table(key, part):
    key = jax.random.fold_in(key, 31)
    block_keys = jax.random.split(key, REQS // REQ_DEV)
    orders = jax.vmap(shuffled)(block_keys)
    return orders.reshape(REQS, MAXP).astype(jnp.int32)


def draw_lengths(key, part):
    key = jax.random.fold_in(key, 41)
    key_len, key_pos = jax.random.split(key)
    drawn = jax.random.randint(key_len, (REQS,), PAGE + 1, MAXP * PAGE + 1)
    longest = jax.random.randint(key_pos, (), 0, REQS)
    return jnp.where(jnp.arange(REQS) == longest, MAXP * PAGE, drawn).astype(jnp.int32)


def with_ends(entries, key, smallest, high):
    longest = entries.shape.index(max(entries.shape))
    spots = []
    for shift in (0, 1):
        where = [jax.random.randint(jax.random.fold_in(key, axis), (), 0, length) for axis, length in enumerate(entries.shape)]
        where[longest] = (where[longest] + shift) % entries.shape[longest]
        spots.append(tuple(where))
    return entries.at[spots[0]].set(smallest).at[spots[1]].set(high)


def block_scale(key, dims, cuts, least, high):
    loudness = 1.0
    for position, parts in cuts:
        heights = jax.random.uniform(jax.random.fold_in(jax.random.fold_in(key, 6), position), (parts,), jnp.float32, least / len(cuts), high / len(cuts))
        loudness = loudness * jnp.repeat(jnp.exp(heights), dims[position] // parts).reshape((-1,) + (1,) * (len(dims) - 1 - position))
    return loudness


def profile(amount, total, bound, slope):
    weights = [(1 << 20) // math.isqrt(standing ** slope) + 1 for standing in range(2, amount + 1)]
    surplus, given = total - bound - (amount - 1), [1] * (amount - 1)
    while surplus > 0:
        candidates = [i for i in range(amount - 1) if given[i] < bound]
        mass, budget = sum([weights[i] for i in candidates]), surplus
        for i in candidates:
            extra = min(bound - given[i], max(1, budget * weights[i] // mass), surplus)
            given[i] = given[i] + extra
            surplus = surplus - extra
    return np.array([bound] + given)


def uneven(rng, number_of, total, bound, skew):
    if number_of == 2:
        one = jax.random.randint(rng, (), max(1, total - bound), min(bound, total - 1) + 1)
        return jnp.stack([one, total - one])
    sizes = jnp.asarray(profile(number_of, total, bound, skew), jnp.int32)
    twos = (number_of - 1) // 2
    giver, sink = sizes[1:1 + 2 * twos:2], sizes[2:2 + 2 * twos:2]
    margin = jnp.minimum(giver - 1, bound - sink)
    shifted = jax.random.randint(jax.random.fold_in(rng, 1), (twos,), 0, 1 << 20) % (margin + 1)
    sizes = sizes.at[1:1 + 2 * twos:2].set(giver - shifted).at[2:2 + 2 * twos:2].set(sink + shifted)
    return sizes[jax.random.permutation(jax.random.fold_in(rng, 2), number_of)]


def routed_block(own_key, own, number, rows, number_of, top, most, lean):
    order = jax.random.permutation(own_key, number_of)
    heavy_load, ordinary = shares(number_of, rows * top, most, lean, True), shares(number_of, rows * top, most, lean, False)
    places = jnp.arange(number_of)

    def named(tallies, turn):
        used = int((tallies > 0).sum())
        fixed = max(1, used // 4)
        passed = fixed + (places - fixed + turn * (used - fixed)) % max(1, number_of - fixed)
        return jnp.zeros((number_of,), jnp.int32).at[order[jnp.where(places < fixed, places, passed)]].set(jnp.asarray(tallies, jnp.int32))

    tallies = jnp.where(number % 4 == 0, named(heavy_load, number // 4), named(ordinary, number - number // 4 - 1))
    mixed = jax.random.permutation(jax.random.fold_in(own, 3), number_of)
    source_of, sink = mixed[0:number_of // 2 * 2:2], mixed[1:number_of // 2 * 2:2]
    margin = jnp.minimum(tallies[source_of] - 1, most - tallies[sink]) // 2
    margin = jnp.where((source_of == order[0]) | (sink == order[0]) | (tallies[sink] == 0), 0, jnp.maximum(margin, 0))
    passed = jax.random.randint(jax.random.fold_in(own, 4), (number_of // 2,), 0, 1 << 20) % (margin + 1)
    tallies = tallies.at[source_of].add(-passed).at[sink].add(passed)
    members = jnp.searchsorted(jnp.cumsum(tallies), jnp.arange(rows * top), side="right").astype(jnp.int32)
    grid = members.reshape(top, rows).T
    grid = grid[jax.random.permutation(jax.random.fold_in(own, 1), rows)]
    turn = jax.random.randint(jax.random.fold_in(own, 2), (rows, 1), 0, top)
    return jnp.take_along_axis(grid, (jnp.arange(top)[None, :] + turn) % top, axis=1)


def shares(count, total, limit, skew, full):
    loads = [(1 << 20) // math.isqrt(rank ** skew) + 1 for rank in range(1, count + 1)]
    largest = limit if full else min(limit, max(-(-total // count), total * loads[0] // sum(loads)))
    least = 1 if total - largest >= count - 1 else 0
    given, surplus = [largest] + [least] * (count - 1), total - largest - least * (count - 1)
    while surplus > 0:
        movable = [i for i in range(1, count) if given[i] < largest] or [i for i in range(1, count) if given[i] < limit]
        pool, budget = sum([loads[i] for i in movable]), surplus
        for i in movable:
            more = min(limit - given[i], max(1, budget * loads[i] // pool), surplus)
            given[i] = given[i] + more
            surplus = surplus - more
    return np.array(given)


def noise(stream_key, shape, spread, reach, cuts=(), kind=jnp.bfloat16):
    values = jax.random.normal(stream_key, shape, jnp.float32) * spread
    if len(cuts) > 0:
        values = block_scale(stream_key, shape, cuts, -0.22, 0.18) * values
    return jnp.clip(values, min=-reach, max=reach).astype(kind)


def setup_inputs(seed: int = 0) -> dict:
    key_of = jax.random.split(jax.random.key(seed), 13)
    queries = draw_queries(jax.random.fold_in(key_of[12], 71), 0)
    resident_kv = draw_resident_kv(jax.random.fold_in(key_of[12], 71), 0)
    swap_kv = draw_swap_kv(jax.random.fold_in(key_of[12], 71), 0)
    page_table = draw_page_table(jax.random.fold_in(key_of[12], 71), 0)
    lengths = draw_lengths(jax.random.fold_in(key_of[12], 71), 0)
    resume_source_keys = jax.random.split(jax.random.fold_in(key_of[5], 1), RESUMED // RES_ROWS)
    resume_source_turns = jax.random.permutation(jax.random.fold_in(key_of[5], 3), RESUMED // RES_ROWS)
    resume_source = jax.vmap(lambda own, number: routed_block(jax.random.fold_in(key_of[5], 2), own, number, RES_ROWS, N_REQ, 1, CAPK, 2))(resume_source_keys, resume_source_turns).reshape((RESUMED, 1))
    resume_page = with_ends(jax.random.randint(key_of[6], (RESUMED,), 0, SWAP_PAGES), jax.random.fold_in(key_of[6], 1), 0, SWAP_PAGES - 1).astype(jnp.int32)
    seg_lengths = jax.vmap(lambda own: uneven(own, SEGS, REQ_DEV, SEGMAX, 1))(jax.random.split(key_of[7], N_REQ)).reshape((N_REQ, SEGS)).astype(jnp.int32)
    segment_adapter_holder_keys = jax.random.split(jax.random.fold_in(key_of[8], 1), SEG_ALL // SEGS)
    segment_adapter_holder_turns = jax.random.permutation(jax.random.fold_in(key_of[8], 3), SEG_ALL // SEGS)
    segment_adapter_holder = jax.vmap(lambda own, number: routed_block(jax.random.fold_in(key_of[8], 2), own, number, SEGS, N_REQ, 1, CAPA, 2))(segment_adapter_holder_keys, segment_adapter_holder_turns).reshape((SEG_ALL, 1))
    seg_slot = with_ends(jax.random.randint(key_of[9], (SEG_ALL,), 0, ADP_DEV), jax.random.fold_in(key_of[9], 1), 0, ADP_DEV - 1).astype(jnp.int32)
    adapter_down = noise(key_of[10], (ADAPTERS, R, D), D ** -0.5, 0.0625, ((0, 32), (2, 8)))
    adapter_up = noise(key_of[11], (ADAPTERS, R, D), R ** -0.5, 0.75, ((0, 32), (2, 8)))
    return dict(queries=queries, resident_kv=resident_kv, swap_kv=swap_kv, page_table=page_table, lengths=lengths, resume_source=resume_source, resume_page=resume_page, seg_lengths=seg_lengths, segment_adapter_holder=segment_adapter_holder, seg_slot=seg_slot, adapter_down=adapter_down, adapter_up=adapter_up)


low_rank_scale = 2.0


def attend(queries, page_space, req_table, req_lengths):
    req_count = queries.shape[0]
    positions = MAXP * PAGE
    picked = page_space[req_table].reshape(req_count, positions, KVH, 2, HD)
    key_rows = picked[:, :, :, 0, :].astype(jnp.float32)
    value_rows = picked[:, :, :, 1, :].astype(jnp.float32)
    head_rows = queries.reshape(req_count, KVH, QH // KVH, HD).astype(jnp.float32)
    scores = jnp.einsum("rkgd,rtkd->rkgt", head_rows, key_rows, precision=lax.Precision.HIGHEST) * (HD ** -0.5)
    live_mask = jnp.arange(positions, dtype=jnp.int32)[None, :] < req_lengths[:, None]
    scores = jnp.where(live_mask[:, None, None, :], scores, -1e30)
    row_top = jnp.max(scores, axis=-1, keepdims=True)
    weights = jnp.exp(scores - row_top)
    probabilities = (weights / jnp.sum(weights, axis=-1, keepdims=True)).astype(jnp.bfloat16)
    mixed = jnp.einsum("rkgt,rtkd->rkgd", probabilities.astype(jnp.float32), value_rows, precision=lax.Precision.HIGHEST)
    return mixed.reshape(req_count, QH * HD).astype(jnp.bfloat16)


def reference(queries, resident_kv, swap_kv, page_table, lengths, resume_source, resume_page, seg_lengths, segment_adapter_holder, seg_slot, adapter_down, adapter_up):
    def serve(device):
        device = device.astype(jnp.int32)
        query_rows = lax.dynamic_slice_in_dim(queries, device * REQ_DEV, REQ_DEV, 0)
        req_table = lax.dynamic_slice_in_dim(page_table, device * REQ_DEV, REQ_DEV, 0)
        req_lengths = lax.dynamic_slice_in_dim(lengths, device * REQ_DEV, REQ_DEV, 0)
        resident = lax.dynamic_slice_in_dim(resident_kv, device * POOL, POOL, 0)
        sources = lax.dynamic_slice_in_dim(resume_source[:, 0], device * RES_ROWS, RES_ROWS, 0)
        wanted = lax.dynamic_slice_in_dim(resume_page, device * RES_ROWS, RES_ROWS, 0)
        arrived = swap_kv[(sources * SWAP_PAGES + wanted).astype(jnp.int32)]
        page_space = jnp.concatenate([resident, arrived], 0)
        mixed = attend(query_rows, page_space, req_table, req_lengths)
        sizes_row = lax.dynamic_index_in_dim(seg_lengths, device, 0, keepdims=False)
        seg_ends = jnp.cumsum(sizes_row)
        positions = jnp.arange(REQ_DEV, dtype=jnp.int32)
        member = jnp.sum((positions[:, None] >= seg_ends[None, :]).astype(jnp.int32), axis=1)
        owners = lax.dynamic_slice_in_dim(segment_adapter_holder[:, 0], device * SEGS, SEGS, 0)
        slot_ids = lax.dynamic_slice_in_dim(seg_slot, device * SEGS, SEGS, 0)
        adapter = (owners * ADP_DEV + slot_ids).astype(jnp.int32)
        downs = adapter_down[adapter].astype(jnp.float32)
        up_weights = adapter_up[adapter].astype(jnp.float32)
        lowered = jnp.einsum("rh,skh->rsk", mixed.astype(jnp.float32), downs, precision=lax.Precision.HIGHEST)
        select = member[:, None] == jnp.arange(SEGS, dtype=jnp.int32)[None, :]
        down_projected = jnp.sum(jnp.where(select[:, :, None], lowered, 0.0), axis=1).astype(jnp.bfloat16)
        up_projected = jnp.where(select[:, :, None], down_projected.astype(jnp.float32)[:, None, :], 0.0)
        adapter_increment = jnp.einsum("jfv,fvx->jx", up_projected, up_weights, precision=lax.Precision.HIGHEST) * low_rank_scale
        return mixed, adapter_increment.astype(jnp.bfloat16), arrived

    mixed, adapter_increment, arrived = lax.map(serve, jnp.arange(N_REQ, dtype=jnp.int32))
    return mixed.reshape(REQS, D), adapter_increment.reshape(REQS, D), arrived.reshape(RESUMED, PAGE, 2 * KVH * HD)
```

```python
import jax
import jax.numpy as jnp
from jax import lax
from jax.sharding import PartitionSpec as P

HD = 128
SEGMAX = 4


low_rank_scale = 2.0


def earlier_same(owner_ids, devices):
    marks = (owner_ids[:, :, None] == jnp.arange(devices, dtype=jnp.int32)[None, None, :]).astype(
        jnp.int32
    )
    before = jnp.cumsum(marks, axis=1) - marks
    return jnp.sum(before * marks, axis=2)


def pack_table(owner_ids, owner_rank, entries, source, capacity):
    places = jnp.arange(capacity, dtype=jnp.int32)
    matches = (owner_ids == source)[:, :, None] & (owner_rank[:, :, None] == places[None, None, :])
    return jnp.sum(jnp.where(matches, entries[:, :, None], 0), axis=1)


def attend(queries, page_space, req_table, req_lengths):
    req_count, width = queries.shape
    kv_heads = page_space.shape[2] // (2 * HD)
    group_size = width // (kv_heads * HD)
    positions = req_table.shape[1] * page_space.shape[1]
    picked = page_space[req_table].reshape(req_count, positions, kv_heads, 2, HD)
    head_rows = queries.reshape(req_count, kv_heads, group_size, HD)
    scores = jnp.einsum(
        "rkgd,rtkd->rkgt", head_rows, picked[:, :, :, 0, :], preferred_element_type=jnp.float32
    ) * HD ** (-0.5)
    live_mask = jnp.arange(positions, dtype=jnp.int32)[None, :] < req_lengths[:, None]
    scores = jnp.where(live_mask[:, None, None, :], scores, -1e30)
    row_top = jnp.max(scores, axis=-1, keepdims=True)
    weights = jnp.exp(scores - row_top)
    probabilities = (weights / jnp.sum(weights, axis=-1, keepdims=True)).astype(jnp.bfloat16)
    mixed = jnp.einsum(
        "rkgt,rtkd->rkgd", probabilities, picked[:, :, :, 1, :], preferred_element_type=jnp.float32
    )
    return mixed.reshape(req_count, width).astype(jnp.bfloat16)


def local(
    queries,
    resident_kv,
    swap_kv,
    page_table,
    lengths,
    resume_source,
    resume_page,
    seg_lengths,
    segment_adapter_holder,
    seg_slot,
    adapter_down,
    adapter_up,
):
    devices = lax.axis_size("req")
    own_index = lax.axis_index("req")
    req_count = queries.shape[0]
    res_rows = resume_page.shape[0] // devices
    res_cap = max(2, 2 * res_rows // devices)
    res_owner = resume_source[:, 0].reshape(devices, res_rows)
    res_rank = earlier_same(res_owner, devices)
    send_page = pack_table(
        res_owner, res_rank, resume_page.reshape(devices, res_rows), own_index, res_cap
    )
    arriving = lax.all_to_all(swap_kv[send_page], "req", split_axis=0, concat_axis=0, tiled=True)
    my_res_owner = lax.dynamic_index_in_dim(res_owner, own_index, 0, keepdims=False)
    my_res_rank = lax.dynamic_index_in_dim(res_rank, own_index, 0, keepdims=False)
    arrived = arriving.reshape((devices * res_cap,) + arriving.shape[2:])[
        my_res_owner * res_cap + my_res_rank
    ]
    page_space = jnp.concatenate([resident_kv, arrived], 0)
    mixed = attend(queries, page_space, page_table, lengths)
    segs = seg_lengths.shape[1]
    rank = adapter_down.shape[1]
    slots = adapter_down.shape[0]
    width = queries.shape[1]
    sizes_row = seg_lengths[0]
    seg_ends = jnp.cumsum(sizes_row)
    seg_starts = seg_ends - sizes_row
    positions = jnp.arange(req_count, dtype=jnp.int32)
    member = jnp.sum((positions[:, None] >= seg_ends[None, :]).astype(jnp.int32), axis=1)
    within = positions - seg_starts[member]
    seg_cap = max(2, 2 * segs // devices)
    owners = segment_adapter_holder[:, 0].reshape(devices, segs)
    owner_rank = earlier_same(owners, devices)
    slots_all = seg_slot.reshape(devices, segs)
    my_owner = lax.dynamic_index_in_dim(owners, own_index, 0, keepdims=False)
    my_rank = lax.dynamic_index_in_dim(owner_rank, own_index, 0, keepdims=False)
    held_slot = pack_table(owners, owner_rank, slots_all, own_index, seg_cap)
    place = ((my_owner * seg_cap + my_rank)[member]) * SEGMAX + within
    rows_out = devices * seg_cap * SEGMAX
    put = (jnp.arange(rows_out, dtype=jnp.int32)[:, None] == place[None, :]).astype(jnp.bfloat16)
    rows = jnp.dot(put, mixed, preferred_element_type=jnp.float32).astype(jnp.bfloat16)
    rows = lax.all_to_all(
        rows.reshape(devices, seg_cap * SEGMAX, width), "req", split_axis=0, concat_axis=0, tiled=True
    ).reshape(rows_out, width)
    row_slot = jnp.repeat(held_slot.reshape(-1), SEGMAX)
    pick = row_slot[:, None] == jnp.arange(slots, dtype=jnp.int32)[None, :]
    shrunk = jnp.einsum(
        "nh,srh->nsr", rows, adapter_down, preferred_element_type=jnp.float32
    )
    shrunk = jnp.sum(jnp.where(pick[:, :, None], shrunk, 0.0), axis=1)
    shrunk = lax.psum(shrunk, "tp").astype(jnp.bfloat16)
    spread = jnp.where(pick[:, :, None], shrunk[:, None, :], jnp.zeros((), jnp.bfloat16))
    delta = (
        jnp.dot(
            spread.reshape(rows_out, slots * rank),
            adapter_up.reshape(slots * rank, width),
            preferred_element_type=jnp.float32,
        )
        * low_rank_scale
    ).astype(jnp.bfloat16)
    back = lax.all_to_all(
        delta.reshape(devices, seg_cap * SEGMAX, width), "req", split_axis=0, concat_axis=0, tiled=True
    ).reshape(rows_out, width)
    adapter_increment = back[place]
    return (mixed, adapter_increment, arrived)


def solution(mesh):
    return jax.shard_map(
        local,
        mesh=mesh,
        in_specs=(
            P("req", "tp"),
            P("req", None, "tp"),
            P("req", None, "tp"),
            P("req", None),
            P("req"),
            P(),
            P(),
            P("req", None),
            P(),
            P(),
            P("req", None, "tp"),
            P("req", None, "tp"),
        ),
        out_specs=(P("req", "tp"), P("req", "tp"), P("req", None, "tp")),
        check_vma=False,
    )
```

```python
import functools

import jax
import jax.numpy as jnp
from jax import lax
from jax.experimental import pallas as pl
from jax.experimental.pallas import tpu as pltpu
from jax.sharding import PartitionSpec as P

HD = 128
SEGMAX = 4
LANES = 128
MESH = pl.DeviceIdType.MESH
NEG = -1e30

low_rank_scale = 2.0


def earlier_same(owner_ids, devices):
    marks = (owner_ids[:, :, None] == jnp.arange(devices, dtype=jnp.int32)[None, None, :]).astype(
        jnp.int32
    )
    before = jnp.cumsum(marks, axis=1) - marks
    return jnp.sum(before * marks, axis=2)


def pack_table(owner_ids, owner_rank, entries, source, capacity):
    places = jnp.arange(capacity, dtype=jnp.int32)
    matches = (owner_ids == source)[:, :, None] & (owner_rank[:, :, None] == places[None, None, :])
    return jnp.sum(jnp.where(matches, entries[:, :, None], 0), axis=1)


def attend_kernel(
    pool, table, lens, place, q_ref, resident, recv, out_ref, arrived, space, qs, att, sem, asem
):
    reqs, width = q_ref.shape
    heads = width // HD
    page = space.shape[1]
    maxp = table.shape[0] // reqs
    span = maxp * page
    news = place.shape[0]
    load_a = pltpu.make_async_copy(resident, space.at[pl.ds(0, pool)], sem.at[0])
    load_b = pltpu.make_async_copy(recv, space.at[pl.ds(pool, recv.shape[0])], sem.at[1])
    load_a.start()
    load_b.start()
    qs[...] = jnp.zeros_like(qs)
    for h in range(heads):
        qs[pl.ds(h, reqs, stride=8), :] = q_ref[:, h * HD : (h + 1) * HD].astype(jnp.float32)
    load_b.wait()

    def put(j, c):
        pltpu.make_async_copy(space.at[pool + place[j]], arrived.at[j], asem).start()
        return c

    lax.fori_loop(0, news, put, 0)
    load_a.wait()
    step = 8

    def body(b, c):
        scores, values = [], []
        for i in range(step):
            r = b * step + i
            at = [table[r * maxp + k] for k in range(maxp)]
            keys = jnp.concatenate([space[a, :, :HD] for a in at], axis=0)
            q = qs[pl.ds(pl.multiple_of(r * 8, 8), 8), :].astype(jnp.bfloat16)
            s = lax.dot_general(
                q, keys, (((1,), (1,)), ((), ())), preferred_element_type=jnp.float32
            ) * (HD ** (-0.5))
            pos = lax.broadcasted_iota(jnp.int32, s.shape, 1)
            scores.append(jnp.where(pos < lens[r], s, NEG))
            values.append(at)
        s = jnp.concatenate(scores, axis=0)
        e = jnp.exp(s - jnp.max(s, axis=1, keepdims=True))
        p = e / jnp.sum(e, axis=1, keepdims=True)
        for i in range(step):
            vals = jnp.concatenate([space[a, :, HD:] for a in values[i]], axis=0)
            o = jnp.dot(
                p[i * 8 : (i + 1) * 8].astype(jnp.bfloat16),
                vals,
                preferred_element_type=jnp.float32,
            )
            att[pl.ds(pl.multiple_of((b * step + i) * 8, 8), 8), :] = o
        return c

    lax.fori_loop(0, reqs // step, body, 0)
    for h in range(heads):
        out_ref[:, h * HD : (h + 1) * HD] = att[pl.ds(h, reqs, stride=8), :].astype(jnp.bfloat16)

    def done(j, c):
        pltpu.make_async_copy(space.at[pool + place[j]], arrived.at[j], asem).wait()
        return c

    lax.fori_loop(0, news, done, 0)


def attend(queries, resident, recv, table, lens, place):
    reqs, width = queries.shape
    pool, page, kvw = resident.shape
    smem = pl.BlockSpec(memory_space=pltpu.SMEM)
    vmem = pl.BlockSpec(memory_space=pltpu.VMEM)
    hbm = pl.BlockSpec(memory_space=pl.ANY)
    return pl.pallas_call(
        functools.partial(attend_kernel, pool),
        out_shape=(
            jax.ShapeDtypeStruct((reqs, width), jnp.bfloat16),
            jax.ShapeDtypeStruct((place.shape[0], page, kvw), jnp.bfloat16),
        ),
        in_specs=[smem, smem, smem, vmem, hbm, hbm],
        out_specs=(vmem, hbm),
        scratch_shapes=[
            pltpu.VMEM((pool + recv.shape[0], page, kvw), jnp.bfloat16),
            pltpu.VMEM((reqs * 8, LANES), jnp.float32),
            pltpu.VMEM((reqs * 8, LANES), jnp.float32),
            pltpu.SemaphoreType.DMA((2,)),
            pltpu.SemaphoreType.DMA,
        ],
        compiler_params=pltpu.CompilerParams(vmem_limit_bytes=40 << 20),
        name="attend",
    )(table, lens, place, queries, resident, recv)


def chain_kernel(
    n, tps, place, held, mix, down, up, out_ref,
    send, got, back, fin, part, parts, ss, rs, sb, rb, st, rt,
):
    reqs, width = mix.shape
    heads = width // HD
    slots, rank = down.shape[0], down.shape[1]
    rows = n * 8
    me, tp = lax.axis_index("req"), lax.axis_index("tp")
    barrier = pltpu.get_barrier_semaphore()

    def hello(d, c):
        pl.semaphore_signal(
            barrier, inc=1, device_id={"req": lax.rem(me + d, n)}, device_id_type=MESH
        )
        return c

    lax.fori_loop(1, n, hello, 0)
    for d in range(1, tps):
        pl.semaphore_signal(
            barrier, inc=1, device_id={"tp": lax.rem(tp + d, tps)}, device_id_type=MESH
        )

    slot_of = lax.broadcasted_iota(jnp.int32, (rows, reqs), 0)
    put = jnp.where(slot_of == place[...], 1.0, 0.0).astype(jnp.bfloat16)
    g = jnp.dot(put, mix[...], preferred_element_type=jnp.float32)
    zero = jnp.zeros((8, LANES), jnp.float32)
    for d in range(n):
        block = [g[d * 8 : (d + 1) * 8, h * HD : (h + 1) * HD] for h in range(heads)]
        block += [zero] * (8 - heads)
        send[d] = jnp.concatenate(block, axis=0).astype(jnp.bfloat16)
    pl.semaphore_wait(barrier, n - 1 + tps - 1)

    def go(src, dst, s_sem, r_sem):
        def start(d, c):
            to = lax.rem(me + d, n)
            pltpu.make_async_remote_copy(
                src_ref=src.at[to], dst_ref=dst.at[me], send_sem=s_sem.at[d], recv_sem=r_sem.at[d],
                device_id={"req": to}, device_id_type=MESH,
            ).start()
            return c

        lax.fori_loop(1, n, start, 0)

    def finish(src, dst, s_sem, r_sem):
        def wait(d, c):
            to = lax.rem(me + d, n)
            frm = lax.rem(me + n - d, n)
            pltpu.make_async_remote_copy(
                src_ref=src.at[to], dst_ref=dst.at[frm], send_sem=s_sem.at[d], recv_sem=r_sem.at[d],
                device_id={"req": to}, device_id_type=MESH,
            ).wait()
            return c

        lax.fori_loop(1, n, wait, 0)

    go(send, got, ss, rs)
    got[me] = send[me]
    finish(send, got, ss, rs)

    x = got[...].astype(jnp.float32)
    a = jnp.concatenate(
        [x[:, h * 8 : (h + 1) * 8, :].reshape(rows, LANES) for h in range(heads)], axis=1
    ).astype(jnp.bfloat16)
    lane = lax.broadcasted_iota(jnp.int32, (rows, LANES), 1)
    per = LANES // rank
    hs = held[...]
    total = jnp.zeros((rows, LANES), jnp.float32)
    for c in range(slots // per):
        w = down[c * per : (c + 1) * per].reshape(per * rank, width)
        s = lax.dot_general(a, w, (((1,), (1,)), ((), ())), preferred_element_type=jnp.float32)
        total = total + jnp.where(hs == c * per + lane // rank, s, 0.0)
    total = total + pltpu.roll(total, rank, 1)
    half = rows // 2
    low = lax.broadcasted_iota(jnp.int32, (half, LANES), 1) < rank
    part[...] = jnp.where(low, total[:half], total[half:])
    copies = []
    for d in range(1, tps):
        copies.append(
            pltpu.make_async_remote_copy(
                src_ref=part, dst_ref=parts.at[d - 1], send_sem=st.at[d - 1], recv_sem=rt.at[d - 1],
                device_id={"tp": lax.rem(tp + d, tps)}, device_id_type=MESH,
            )
        )
        copies[-1].start()
    for copy in copies:
        copy.wait()
    acc = part[...]
    for d in range(tps - 1):
        acc = acc + parts[d]
    turned = pltpu.roll(acc, rank, 1)
    shrunk = jnp.concatenate(
        [jnp.where(low, acc, turned), jnp.where(low, turned, acc)], axis=0
    ).astype(jnp.bfloat16)
    spread = jnp.concatenate(
        [
            jnp.where(hs == c * per + lane // rank, shrunk, jnp.zeros((), jnp.bfloat16))
            for c in range(slots // per)
        ],
        axis=1,
    )
    for h in range(heads):
        w = up[:, :, h * HD : (h + 1) * HD].reshape(slots * rank, HD)
        t = jnp.dot(spread, w, preferred_element_type=jnp.float32) * low_rank_scale
        t = t.astype(jnp.bfloat16).astype(jnp.float32)
        part2 = t.reshape(n, 8, LANES)
        fin[:, h * 8 : (h + 1) * 8, :] = part2
    fin[:, heads * 8 :, :] = jnp.zeros((n, 64 - heads * 8, LANES), jnp.float32)
    send[...] = fin[...].astype(jnp.bfloat16)
    go(send, back, sb, rb)
    back[me] = send[me]
    finish(send, back, sb, rb)
    y = back[...].astype(jnp.float32)
    b = jnp.concatenate(
        [y[:, h * 8 : (h + 1) * 8, :].reshape(rows, LANES) for h in range(heads)], axis=1
    ).astype(jnp.bfloat16)
    out_ref[...] = lax.dot_general(
        put, b, (((0,), (0,)), ((), ())), preferred_element_type=jnp.float32
    ).astype(jnp.bfloat16)


def chain(n, tps, place, held, mixed, down, up):
    reqs, width = mixed.shape
    vmem = pl.BlockSpec(memory_space=pltpu.VMEM)
    dma = pltpu.SemaphoreType.DMA
    rows = n * 8
    return pl.pallas_call(
        functools.partial(chain_kernel, n, tps),
        out_shape=jax.ShapeDtypeStruct((reqs, width), jnp.bfloat16),
        in_specs=[vmem] * 5,
        out_specs=vmem,
        scratch_shapes=[
            pltpu.VMEM((n, 64, LANES), jnp.bfloat16),
            pltpu.VMEM((n, 64, LANES), jnp.bfloat16),
            pltpu.VMEM((n, 64, LANES), jnp.bfloat16),
            pltpu.VMEM((n, 64, LANES), jnp.float32),
            pltpu.VMEM((rows // 2, LANES), jnp.float32),
            pltpu.VMEM((tps - 1, rows // 2, LANES), jnp.float32),
            dma((n,)), dma((n,)), dma((n,)), dma((n,)), dma((tps - 1,)), dma((tps - 1,)),
        ],
        compiler_params=pltpu.CompilerParams(
            collective_id=0, has_side_effects=True, vmem_limit_bytes=40 << 20
        ),
        name="chain",
    )(place, held, mixed, down, up)


def local(
    queries,
    resident_kv,
    swap_kv,
    page_table,
    lengths,
    resume_source,
    resume_page,
    seg_lengths,
    segment_adapter_holder,
    seg_slot,
    adapter_down,
    adapter_up,
):
    devices = lax.axis_size("req")
    tps = lax.axis_size("tp")
    own_index = lax.axis_index("req")
    req_count = queries.shape[0]
    pool = resident_kv.shape[0]
    res_rows = resume_page.shape[0] // devices
    res_cap = max(2, 2 * res_rows // devices)
    res_owner = resume_source[:, 0].reshape(devices, res_rows)
    res_rank = earlier_same(res_owner, devices)
    send_page = pack_table(
        res_owner, res_rank, resume_page.reshape(devices, res_rows), own_index, res_cap
    )
    arriving = lax.all_to_all(swap_kv[send_page], "req", split_axis=0, concat_axis=0, tiled=True)
    my_res_owner = lax.dynamic_index_in_dim(res_owner, own_index, 0, keepdims=False)
    my_res_rank = lax.dynamic_index_in_dim(res_rank, own_index, 0, keepdims=False)
    recv = arriving.reshape((devices * res_cap,) + arriving.shape[2:])
    place_res = my_res_owner * res_cap + my_res_rank
    flat = page_table.reshape(-1)
    where_new = jnp.sum(
        jnp.where(
            flat[:, None] - pool == jnp.arange(res_rows, dtype=jnp.int32)[None, :], place_res[None, :], 0
        ),
        axis=1,
    )
    table = jnp.where(flat < pool, flat, pool + where_new)
    mixed, arrived = attend(queries, resident_kv, recv, table, lengths, place_res)

    segs = seg_lengths.shape[1]
    sizes_row = seg_lengths[0]
    seg_ends = jnp.cumsum(sizes_row)
    seg_starts = seg_ends - sizes_row
    positions = jnp.arange(req_count, dtype=jnp.int32)
    member = jnp.sum((positions[:, None] >= seg_ends[None, :]).astype(jnp.int32), axis=1)
    within = positions - seg_starts[member]
    seg_cap = max(2, 2 * segs // devices)
    owners = segment_adapter_holder[:, 0].reshape(devices, segs)
    owner_rank = earlier_same(owners, devices)
    slots_all = seg_slot.reshape(devices, segs)
    my_owner = lax.dynamic_index_in_dim(owners, own_index, 0, keepdims=False)
    my_rank = lax.dynamic_index_in_dim(owner_rank, own_index, 0, keepdims=False)
    held_slot = pack_table(owners, owner_rank, slots_all, own_index, seg_cap)
    place = ((my_owner * seg_cap + my_rank)[member]) * SEGMAX + within
    row_slot = jnp.repeat(held_slot.reshape(-1), SEGMAX)[:, None]
    adapter_increment = chain(
        devices, tps, place[None, :], row_slot, mixed, adapter_down, adapter_up
    )
    return (mixed, adapter_increment, arrived)


def solution(mesh):
    return jax.shard_map(
        local,
        mesh=mesh,
        in_specs=(
            P("req", "tp"),
            P("req", None, "tp"),
            P("req", None, "tp"),
            P("req", None),
            P("req"),
            P(),
            P(),
            P("req", None),
            P(),
            P(),
            P("req", None, "tp"),
            P("req", None, "tp"),
        ),
        out_specs=(P("req", "tp"), P("req", "tp"), P("req", None, "tp")),
        check_vma=False,
    )
```

```python
import functools

import jax
import jax.numpy as jnp
from jax import lax
from jax.experimental import pallas as pl
from jax.experimental.pallas import tpu as pltpu
from jax.sharding import PartitionSpec as P

HD = 128
SEGMAX = 4
LANES = 128
MESH = pl.DeviceIdType.MESH
NEG = -1e30
RZ, RX = 8, 4
CAP = 4
CHUNK = 8
NEAR = 24
FAR = 8

low_rank_scale = 2.0


def iota(shape, dim):
    return lax.broadcasted_iota(jnp.int32, shape, dim)


def ones(mask):
    return jnp.where(mask, 1.0, 0.0)


def mm(a, b):
    return jnp.dot(
        a.astype(jnp.bfloat16), b.astype(jnp.bfloat16), preferred_element_type=jnp.float32
    )


def mmt(a, b):
    return lax.dot_general(
        a.astype(jnp.bfloat16),
        b.astype(jnp.bfloat16),
        (((1,), (1,)), ((), ())),
        preferred_element_type=jnp.float32,
    )


def before(n, block):
    r, c = iota((n, n), 0), iota((n, n), 1)
    return ones((r < c) & (r // block == c // block))


def row_of(x, i):
    return jnp.sum(jnp.where(iota(x.shape, 0) == i, x, jnp.zeros((), x.dtype)), axis=0, keepdims=True)


def ring_plan(source, wanted, zi, xi, stores, pages, per_block):
    shape = (RZ, pages)
    zs = iota(shape, 0)
    need = []
    for zd in range(RZ):
        total = jnp.zeros(shape, jnp.float32)
        for h in range(2):
            s = source[2 * zd + h : 2 * zd + h + 1]
            w = wanted[2 * zd + h : 2 * zd + h + 1]
            a = ones(iota((RZ, LANES), 0) * RX + xi == s)
            b = ones(iota((pages, LANES), 0) == w)
            total = total + mmt(a, b)
        need.append(total)
    at = {}
    for k in (3, 4, 5):
        at[k] = jnp.zeros(shape, jnp.float32)
        for zd in range(RZ):
            at[k] = jnp.where(lax.rem(zd - zs + RZ, RZ) == k, need[zd], at[k])
        at[k] = ones(at[k] > 0.5)
    tri = before(pages, pages)
    far = at[4]
    far_up = far * ones(mm(far, tri) < FAR - 0.5)
    far_down = far - far_up
    lists = {}
    for name, f4, f3 in (("up", far_up, at[3]), ("down", far_down, at[5])):
        f3 = f3 * (1.0 - f4)
        place4 = mm(f4, tri)
        place3 = jnp.sum(f4, axis=1, keepdims=True) + mm(f3, tri)
        lists[name] = (f4, f3, place4, f4 * place4 + f3 * place3)
    page_id = iota(shape, 1).astype(jnp.float32)
    k = lax.rem(zi - zs + RZ, RZ)
    spot4 = jnp.where(far_up > 0.5, lists["up"][2], FAR + lists["down"][2])
    spot = jnp.where(
        k == 3, lists["up"][3], jnp.where(k == 5, lists["down"][3], jnp.where(k == 4, spot4, page_id))
    )
    send = []
    for name, owner in (("up", lax.rem(zi + RZ - 2, RZ)), ("down", lax.rem(zi + 2, RZ))):
        f4, f3, _, place = lists[name]
        used = row_of(f4 + f3, owner)
        p = row_of(place, owner)
        hit = (iota((pages, pages), 0).astype(jnp.float32) == p) & (used > 0.5)
        send.append(
            jnp.sum(
                jnp.where(hit, iota((pages, pages), 1).astype(jnp.float32), 0.0), axis=1, keepdims=True
            )
        )
    tri2 = before(LANES, per_block)
    table = jnp.zeros((RZ, LANES), jnp.float32)
    landing = []
    lane = iota((1, LANES), 1)
    for h in range(2):
        s = row_of(source, 2 * zi + h)
        w = row_of(wanted, 2 * zi + h)
        hot = ones(iota((stores, LANES), 0) == s)
        rank = jnp.sum(hot * mm(hot, tri2), axis=0, keepdims=True)
        landing.append(s.astype(jnp.float32) * CAP + rank)
        v = mm(spot, ones(iota((pages, LANES), 0) == w))
        v = v * ones(iota((RZ, LANES), 0) * RX + xi == s)
        column = (2 * h + lane // per_block) * CAP + rank.astype(jnp.int32)
        table = table + mmt(v, ones(iota((LANES, LANES), 0) == column))
    top = jnp.concatenate(
        [table, landing[0], landing[1], jnp.zeros((RZ - 2, LANES), jnp.float32)], axis=0
    )
    wide = iota((pages, LANES), 1)
    tail = jnp.where(wide == 0, send[0], jnp.where(wide == 1, send[1], 0.0))
    return jnp.concatenate([top, tail], axis=0).astype(jnp.int32)


def chain_plan(n, reqs, sizes, holder, slot, me):
    segs = sizes.shape[1]
    rows = n * 8
    blocks = LANES // segs
    tri = before(LANES, segs)
    mine = ones(holder == me)
    order = mm(mine, tri)
    spread = iota((rows, holder.shape[0]), 0) // (8 * blocks) == iota((rows, holder.shape[0]), 1)
    y = []
    for q in range(2):
        x = jnp.where((mine > 0.5) & (jnp.abs(order - q) < 0.5), slot, 0).astype(jnp.float32)
        y.append(mm(ones(spread), x))
    number = iota((rows, LANES), 0)
    pick = jnp.where(lax.rem(number // 4, 2) == 0, y[0], y[1])
    pick = jnp.where(iota((rows, LANES), 1) // segs == lax.rem(number // 8, blocks), pick, 0.0)
    held = jnp.sum(pick, axis=1, keepdims=True).astype(jnp.int32)

    own = row_of(holder, me // blocks)
    hot = ones(iota((n, LANES), 0) == own)
    rank = jnp.sum(hot * mm(hot, tri), axis=0, keepdims=True)
    value = (own.astype(jnp.float32) * 2 + rank) * SEGMAX
    diag = iota((segs, LANES), 1) == lax.rem(me, blocks) * segs + iota((segs, LANES), 0)
    value = jnp.sum(jnp.where(diag, value, 0.0), axis=1, keepdims=True)
    size = sizes.astype(jnp.float32)
    square = iota((segs, segs), 1) == iota((segs, segs), 0)
    wide = jnp.where(square, size, 0.0)
    size = jnp.sum(wide, axis=1, keepdims=True)
    start = jnp.sum(
        jnp.where(
            iota((segs, segs), 1) < iota((segs, segs), 0), sizes.astype(jnp.float32), 0.0
        ),
        axis=1,
        keepdims=True,
    )
    r = iota((segs, reqs), 1).astype(jnp.float32)
    inside = (r >= start) & (r < start + size)
    place = jnp.sum(jnp.where(inside, value - start + r, 0.0), axis=0, keepdims=True)
    return place.astype(jnp.int32), held


def by_heads(x, rows, heads):
    return jnp.concatenate(
        [x[:, h * 8 : (h + 1) * 8, :].reshape(rows, LANES) for h in range(heads)], axis=1
    )


def main_kernel(
    n, tps,
    table, lens, q_ref, source, wanted, sizes, holder, slot, resident, swap, down_in, up_in,
    out_ref, delta_ref, arrived,
    space, store, near_up, near_down, next_up, next_down, on_up, on_down, third_up, third_down,
    fourth, crossing, arr, qs, att, down, up, send, got, back, fin, part, parts, plan, book,
    load, s1, r1, s2, r2, s3, r3, s4, r4, sx, rx, ss, rs, sb, rb, st, rt,
):
    reqs, width = q_ref.shape
    heads = width // HD
    pool, page = resident.shape[0], resident.shape[1]
    maxp = table.shape[1]
    news = arr.shape[0]
    pages = store.shape[0]
    slots, rank = down.shape[0], down.shape[1]
    rows = n * 8
    me, tp = lax.axis_index("req"), lax.axis_index("tp")
    zi, xi = me // RX, lax.rem(me, RX)
    above = lax.rem(zi + 1, RZ) * RX + xi
    below = lax.rem(zi + RZ - 1, RZ) * RX + xi
    barrier = pltpu.get_barrier_semaphore()

    loads = [
        pltpu.make_async_copy(swap, store, load.at[0]),
        pltpu.make_async_copy(resident, space.at[pl.ds(0, pool)], load.at[1]),
        pltpu.make_async_copy(down_in, down, load.at[2]),
        pltpu.make_async_copy(up_in, up, load.at[3]),
    ]
    loads[0].start()

    def hello(d, c):
        pl.semaphore_signal(
            barrier, inc=1, device_id={"req": lax.rem(me + d, n)}, device_id_type=MESH
        )
        return c

    lax.fori_loop(1, n, hello, 0)
    for d in range(1, tps):
        pl.semaphore_signal(
            barrier, inc=1, device_id={"tp": lax.rem(tp + d, tps)}, device_id_type=MESH
        )
    loads[0].wait()
    pl.semaphore_wait(barrier, n - 1 + tps - 1)

    def hop(src, dst, ssem, rsem, to):
        return pltpu.make_async_remote_copy(
            src_ref=src, dst_ref=dst, send_sem=ssem, recv_sem=rsem,
            device_id={"req": to}, device_id_type=MESH,
        )

    sides = (above, below)
    near, nxt, on, third = (
        (near_up, near_down), (next_up, next_down), (on_up, on_down), (third_up, third_down)
    )

    def part_of(ref, c):
        return ref.at[pl.ds(c * CHUNK, CHUNK)]

    first, second, later, last = [], [], [], []
    for c in range(pages // CHUNK):
        for w in range(2):
            first.append(
                hop(part_of(store, c), part_of(near[w], c), s1.at[w, c], r1.at[w, c], sides[w])
            )
            second.append(
                hop(part_of(near[w], c), part_of(nxt[w], c), s2.at[w, c], r2.at[w, c], sides[w])
            )
    for c in range(NEAR // CHUNK):
        for w in range(2):
            later.append(
                hop(part_of(on[w], c), part_of(third[w], c), s3.at[w, c], r3.at[w, c], sides[w])
            )
    for w in range(2):
        last.append(
            hop(third[w].at[pl.ds(0, FAR)], part_of(fourth, w), s4.at[w], r4.at[w], sides[w])
        )
    for copy in first:
        copy.start()
    for copy in loads[1:]:
        copy.start()

    plan[...] = ring_plan(source[...], wanted[...], zi, xi, n, pages, news)
    enter = pltpu.make_async_copy(plan, book, load.at[0])
    enter.start()
    slot_place, hs = chain_plan(n, reqs, sizes[...], holder[...], slot[...], me)
    put = ones(iota((rows, reqs), 0) == slot_place).astype(jnp.bfloat16)
    qs[...] = jnp.zeros_like(qs)
    for h in range(heads):
        qs[pl.ds(h, reqs, stride=8), :] = q_ref[:, h * HD : (h + 1) * HD].astype(jnp.float32)
    enter.wait()

    def within(i, ref):
        return jnp.clip(i, 0, ref.shape[0] - 1)

    def land(z, x):
        return pool + (z * RX + x) * CAP

    def cross_copy(k, dx):
        z = lax.rem(zi + RZ - k, RZ)
        return hop(
            crossing.at[k, dx - 1], space.at[pl.ds(land(z, xi), CAP)],
            sx.at[k, dx - 1], rx.at[k, dx - 1], z_row(dx),
        )

    def z_row(dx):
        return zi * RX + lax.rem(xi + dx, RX)

    def cross(k, ref):
        z = lax.rem(zi + RZ - k, RZ)
        for dx in (2, 1, 3):
            xd = lax.rem(xi + dx, RX)
            for r in range(CAP):
                crossing[k, dx - 1, r] = ref[within(book[z, xd * CAP + r], ref)]
            cross_copy(k, dx).start()
        for r in range(CAP):
            space[land(z, xi) + r] = ref[within(book[z, xi * CAP + r], ref)]

    cross(0, store)
    for a, b in zip(first, second):
        a.wait_recv()
        b.start()
    cross(1, near_up)
    cross(7, near_down)
    for copy in second:
        copy.wait_recv()
    for w in range(2):
        for c in range(NEAR // CHUNK):
            for i in range(CHUNK):
                on[w][c * CHUNK + i] = nxt[w][within(book[16 + c * CHUNK + i, w], nxt[w])]
            later[c * 2 + w].start()
    cross(2, next_up)
    cross(6, next_down)
    for i, copy in enumerate(later):
        copy.wait_recv()
        if i < 2:
            last[i].start()
    cross(3, third_up)
    cross(5, third_down)
    for copy in last:
        copy.wait_recv()
    cross(4, fourth)
    for copy in loads[1:]:
        copy.wait()
    for copy in first + second + later + last:
        copy.wait_send()
    for k in range(RZ):
        for dx in range(1, RX):
            cross_copy(k, dx).wait_send()
            z = lax.rem(zi + RZ - k, RZ)
            x = lax.rem(xi + RX - dx, RX)
            hop(
                crossing.at[k, dx - 1], space.at[pl.ds(land(z, x), CAP)],
                sx.at[k, dx - 1], rx.at[k, dx - 1], z_row(dx),
            ).wait_recv()

    def spot(j):
        return pool + jnp.clip(book[8 + xi // 2, lax.rem(xi, 2) * news + j], 0, n * CAP - 1)

    def pick(j, c):
        arr[j] = space[spot(j)]
        return c

    lax.fori_loop(0, news, pick, 0)
    keep = pltpu.make_async_copy(arr, arrived, load.at[0])
    keep.start()

    step = 8

    def page_at(r, k):
        t = table[r, k]
        return jnp.where(t < pool, jnp.clip(t, 0, pool - 1), spot(jnp.clip(t - pool, 0, news - 1)))

    def body(b, c):
        scores, spots = [], []
        for i in range(step):
            r = b * step + i
            at = [page_at(r, k) for k in range(maxp)]
            keys = jnp.concatenate([space[a, :, :HD] for a in at], axis=0)
            q = qs[pl.ds(pl.multiple_of(r * 8, 8), 8), :].astype(jnp.bfloat16)
            s = lax.dot_general(
                q, keys, (((1,), (1,)), ((), ())), preferred_element_type=jnp.float32
            ) * (HD ** (-0.5))
            pos = lax.broadcasted_iota(jnp.int32, s.shape, 1)
            scores.append(jnp.where(pos < lens[r], s, NEG))
            spots.append(at)
        s = jnp.concatenate(scores, axis=0)
        e = jnp.exp(s - jnp.max(s, axis=1, keepdims=True))
        p = e / jnp.sum(e, axis=1, keepdims=True)
        for i in range(step):
            vals = jnp.concatenate([space[a, :, HD:] for a in spots[i]], axis=0)
            o = jnp.dot(
                p[i * 8 : (i + 1) * 8].astype(jnp.bfloat16),
                vals,
                preferred_element_type=jnp.float32,
            )
            att[pl.ds(pl.multiple_of((b * step + i) * 8, 8), 8), :] = o
        return c

    lax.fori_loop(0, reqs // step, body, 0)
    for h in range(heads):
        out_ref[:, h * HD : (h + 1) * HD] = att[pl.ds(h, reqs, stride=8), :].astype(jnp.bfloat16)

    g = jnp.dot(put, out_ref[...], preferred_element_type=jnp.float32)
    zero = jnp.zeros((8, LANES), jnp.float32)

    def go(src, dst, s_sem, r_sem):
        def start(d, c):
            to = lax.rem(me + d, n)
            pltpu.make_async_remote_copy(
                src_ref=src.at[to], dst_ref=dst.at[me], send_sem=s_sem.at[d], recv_sem=r_sem.at[d],
                device_id={"req": to}, device_id_type=MESH,
            ).start()
            return c

        lax.fori_loop(1, n, start, 0)

    def finish(src, dst, s_sem, r_sem):
        def wait(d, c):
            to = lax.rem(me + d, n)
            frm = lax.rem(me + n - d, n)
            pltpu.make_async_remote_copy(
                src_ref=src.at[to], dst_ref=dst.at[frm], send_sem=s_sem.at[d], recv_sem=r_sem.at[d],
                device_id={"req": to}, device_id_type=MESH,
            ).wait()
            return c

        lax.fori_loop(1, n, wait, 0)

    for d in range(n):
        block = [g[d * 8 : (d + 1) * 8, h * HD : (h + 1) * HD] for h in range(heads)]
        block += [zero] * (8 - heads)
        send[d] = jnp.concatenate(block, axis=0).astype(jnp.bfloat16)
    go(send, got, ss, rs)
    got[me] = send[me]
    finish(send, got, ss, rs)

    a = by_heads(got[...].astype(jnp.float32), rows, heads).astype(jnp.bfloat16)
    lane = lax.broadcasted_iota(jnp.int32, (rows, LANES), 1)
    per = LANES // rank
    total = jnp.zeros((rows, LANES), jnp.float32)
    for c in range(slots // per):
        w = down[c * per : (c + 1) * per].reshape(per * rank, width)
        s = lax.dot_general(a, w, (((1,), (1,)), ((), ())), preferred_element_type=jnp.float32)
        total = total + jnp.where(hs == c * per + lane // rank, s, 0.0)
    total = total + pltpu.roll(total, rank, 1)
    half = rows // 2
    low = lax.broadcasted_iota(jnp.int32, (half, LANES), 1) < rank
    part[...] = jnp.where(low, total[:half], total[half:])
    copies = []
    for d in range(1, tps):
        copies.append(
            pltpu.make_async_remote_copy(
                src_ref=part, dst_ref=parts.at[d - 1], send_sem=st.at[d - 1], recv_sem=rt.at[d - 1],
                device_id={"tp": lax.rem(tp + d, tps)}, device_id_type=MESH,
            )
        )
        copies[-1].start()
    for copy in copies:
        copy.wait()
    acc = part[...]
    for d in range(tps - 1):
        acc = acc + parts[d]
    turned = pltpu.roll(acc, rank, 1)
    shrunk = jnp.concatenate(
        [jnp.where(low, acc, turned), jnp.where(low, turned, acc)], axis=0
    ).astype(jnp.bfloat16)
    spread = jnp.concatenate(
        [
            jnp.where(hs == c * per + lane // rank, shrunk, jnp.zeros((), jnp.bfloat16))
            for c in range(slots // per)
        ],
        axis=1,
    )
    for h in range(heads):
        w = up[:, :, h * HD : (h + 1) * HD].reshape(slots * rank, HD)
        t = jnp.dot(spread, w, preferred_element_type=jnp.float32) * low_rank_scale
        fin[:, h * 8 : (h + 1) * 8, :] = t.reshape(n, 8, LANES)
    fin[:, heads * 8 :, :] = jnp.zeros((n, 64 - heads * 8, LANES), jnp.float32)
    send[...] = fin[...].astype(jnp.bfloat16)
    go(send, back, sb, rb)
    back[me] = send[me]
    finish(send, back, sb, rb)
    b = by_heads(back[...].astype(jnp.float32), rows, heads).astype(jnp.bfloat16)
    delta_ref[...] = lax.dot_general(
        put, b, (((0,), (0,)), ((), ())), preferred_element_type=jnp.float32
    ).astype(jnp.bfloat16)
    keep.wait()


def serve(n, tps, table, lens, queries, source, wanted, sizes, holder, slot, resident, swap, down, up):
    reqs, width = queries.shape
    pool, page, kvw = resident.shape
    news = source.size // n
    rows = n * 8
    smem = pl.BlockSpec(memory_space=pltpu.SMEM)
    vmem = pl.BlockSpec(memory_space=pltpu.VMEM)
    hbm = pl.BlockSpec(memory_space=pl.ANY)
    dma = pltpu.SemaphoreType.DMA
    bf16, f32 = jnp.bfloat16, jnp.float32
    stores = swap.shape[0]

    def held(count):
        return pltpu.VMEM((count, page, kvw), bf16)

    return pl.pallas_call(
        functools.partial(main_kernel, n, tps),
        out_shape=(
            jax.ShapeDtypeStruct((reqs, width), bf16),
            jax.ShapeDtypeStruct((reqs, width), bf16),
            jax.ShapeDtypeStruct((news, page, kvw), bf16),
        ),
        in_specs=[smem] * 2 + [vmem] * 6 + [hbm] * 4,
        out_specs=(vmem, vmem, hbm),
        scratch_shapes=[
            held(pool + n * CAP),
            held(stores), held(stores), held(stores), held(stores), held(stores),
            held(NEAR), held(NEAR), held(NEAR), held(NEAR), held(2 * FAR),
            pltpu.VMEM((RZ, RX - 1, CAP, page, kvw), bf16),
            held(news),
            pltpu.VMEM((reqs * 8, LANES), f32),
            pltpu.VMEM((reqs * 8, LANES), f32),
            pltpu.VMEM(down.shape, bf16),
            pltpu.VMEM(up.shape, bf16),
            pltpu.VMEM((n, 64, LANES), bf16),
            pltpu.VMEM((n, 64, LANES), bf16),
            pltpu.VMEM((n, 64, LANES), bf16),
            pltpu.VMEM((n, 64, LANES), f32),
            pltpu.VMEM((rows // 2, LANES), f32),
            pltpu.VMEM((tps - 1, rows // 2, LANES), f32),
            pltpu.VMEM((16 + stores, LANES), jnp.int32),
            pltpu.SMEM((16 + stores, LANES), jnp.int32),
            dma((4,)),
            dma((2, stores // CHUNK)), dma((2, stores // CHUNK)),
            dma((2, stores // CHUNK)), dma((2, stores // CHUNK)),
            dma((2, NEAR // CHUNK)), dma((2, NEAR // CHUNK)), dma((2,)), dma((2,)),
            dma((RZ, RX - 1)), dma((RZ, RX - 1)),
            dma((n,)), dma((n,)), dma((n,)), dma((n,)),
            dma((tps - 1,)), dma((tps - 1,)),
        ],
        compiler_params=pltpu.CompilerParams(
            collective_id=0, has_side_effects=True, vmem_limit_bytes=56 << 20
        ),
        name="serve",
    )(table, lens, queries, source, wanted, sizes, holder, slot, resident, swap, down, up)


def local(
    queries,
    resident_kv,
    swap_kv,
    page_table,
    lengths,
    resume_source,
    resume_page,
    seg_lengths,
    segment_adapter_holder,
    seg_slot,
    adapter_down,
    adapter_up,
):
    return serve(
        lax.axis_size("req"),
        lax.axis_size("tp"),
        page_table,
        lengths,
        queries,
        resume_source.reshape(-1, LANES),
        resume_page.reshape(-1, LANES),
        seg_lengths,
        segment_adapter_holder.reshape(-1, LANES),
        seg_slot.reshape(-1, LANES),
        resident_kv,
        swap_kv,
        adapter_down,
        adapter_up,
    )


def solution(mesh):
    return jax.shard_map(
        local,
        mesh=mesh,
        in_specs=(
            P("req", "tp"),
            P("req", None, "tp"),
            P("req", None, "tp"),
            P("req", None),
            P("req"),
            P(),
            P(),
            P("req", None),
            P(),
            P(),
            P("req", None, "tp"),
            P("req", None, "tp"),
        ),
        out_specs=(P("req", "tp"), P("req", "tp"), P("req", None, "tp")),
        check_vma=False,
    )
```

```python
import functools

import jax
import jax.numpy as jnp
from jax import lax
from jax.experimental import pallas as pl
from jax.experimental.pallas import tpu as pltpu
from jax.sharding import PartitionSpec as P

HD = 128
SEGMAX = 4
LANES = 128
MESH = pl.DeviceIdType.MESH
NEG = -1e30
RZ, RX = 8, 4
CAP = 4
CHUNK = 8
NEAR = 24
FAR = 8

low_rank_scale = 2.0


def iota(shape, dim):
    return lax.broadcasted_iota(jnp.int32, shape, dim)


def ones(mask):
    return jnp.where(mask, 1.0, 0.0)


def mm(a, b):
    return jnp.dot(
        a.astype(jnp.bfloat16), b.astype(jnp.bfloat16), preferred_element_type=jnp.float32
    )


def mmt(a, b):
    return lax.dot_general(
        a.astype(jnp.bfloat16),
        b.astype(jnp.bfloat16),
        (((1,), (1,)), ((), ())),
        preferred_element_type=jnp.float32,
    )


def before(n, block):
    r, c = iota((n, n), 0), iota((n, n), 1)
    return ones((r < c) & (r // block == c // block))


def row_of(x, i):
    return jnp.sum(jnp.where(iota(x.shape, 0) == i, x, jnp.zeros((), x.dtype)), axis=0, keepdims=True)


def ring_plan(source, wanted, zi, xi, stores, pages, per_block):
    shape = (RZ, pages)
    zs = iota(shape, 0)
    need = []
    for zd in range(RZ):
        total = jnp.zeros(shape, jnp.float32)
        for h in range(2):
            s = source[2 * zd + h : 2 * zd + h + 1]
            w = wanted[2 * zd + h : 2 * zd + h + 1]
            a = ones(iota((RZ, LANES), 0) * RX + xi == s)
            b = ones(iota((pages, LANES), 0) == w)
            total = total + mmt(a, b)
        need.append(total)
    at = {}
    for k in (3, 4, 5):
        at[k] = jnp.zeros(shape, jnp.float32)
        for zd in range(RZ):
            at[k] = jnp.where(lax.rem(zd - zs + RZ, RZ) == k, need[zd], at[k])
        at[k] = ones(at[k] > 0.5)
    tri = before(pages, pages)
    far = at[4]
    far_up = far * ones(mm(far, tri) < FAR - 0.5)
    far_down = far - far_up
    lists = {}
    for name, f4, f3 in (("up", far_up, at[3]), ("down", far_down, at[5])):
        f3 = f3 * (1.0 - f4)
        place4 = mm(f4, tri)
        place3 = jnp.sum(f4, axis=1, keepdims=True) + mm(f3, tri)
        lists[name] = (f4, f3, place4, f4 * place4 + f3 * place3)
    page_id = iota(shape, 1).astype(jnp.float32)
    k = lax.rem(zi - zs + RZ, RZ)
    spot4 = jnp.where(far_up > 0.5, lists["up"][2], FAR + lists["down"][2])
    spot = jnp.where(
        k == 3, lists["up"][3], jnp.where(k == 5, lists["down"][3], jnp.where(k == 4, spot4, page_id))
    )
    send = []
    for name, owner in (("up", lax.rem(zi + RZ - 2, RZ)), ("down", lax.rem(zi + 2, RZ))):
        f4, f3, _, place = lists[name]
        used = row_of(f4 + f3, owner)
        p = row_of(place, owner)
        hit = (iota((pages, pages), 0).astype(jnp.float32) == p) & (used > 0.5)
        send.append(
            jnp.sum(
                jnp.where(hit, iota((pages, pages), 1).astype(jnp.float32), 0.0), axis=1, keepdims=True
            )
        )
    tri2 = before(LANES, per_block)
    table = jnp.zeros((RZ, LANES), jnp.float32)
    landing = []
    lane = iota((1, LANES), 1)
    for h in range(2):
        s = row_of(source, 2 * zi + h)
        w = row_of(wanted, 2 * zi + h)
        hot = ones(iota((stores, LANES), 0) == s)
        rank = jnp.sum(hot * mm(hot, tri2), axis=0, keepdims=True)
        landing.append(s.astype(jnp.float32) * CAP + rank)
        v = mm(spot, ones(iota((pages, LANES), 0) == w))
        v = v * ones(iota((RZ, LANES), 0) * RX + xi == s)
        column = (2 * h + lane // per_block) * CAP + rank.astype(jnp.int32)
        table = table + mmt(v, ones(iota((LANES, LANES), 0) == column))
    top = jnp.concatenate(
        [table, landing[0], landing[1], jnp.zeros((RZ - 2, LANES), jnp.float32)], axis=0
    )
    wide = iota((pages, LANES), 1)
    tail = jnp.where(wide == 0, send[0], jnp.where(wide == 1, send[1], 0.0))
    return jnp.concatenate([top, tail], axis=0).astype(jnp.int32)


def apart(p, n):
    return 2 * lax.rem(p, n // 2) + p // (n // 2)


def chain_plan(n, reqs, sizes, holder, slot, me):
    segs = sizes.shape[1]
    rows = n * 8
    blocks = LANES // segs
    tri = before(LANES, segs)
    mine = ones(holder == me)
    order = mm(mine, tri)

    def sender(number):
        return lax.rem(me - apart(number // 8, n) + n, n)

    wide = (rows, holder.shape[0])
    spread = sender(iota(wide, 0)) // blocks == iota(wide, 1)
    y = []
    for q in range(2):
        x = jnp.where((mine > 0.5) & (jnp.abs(order - q) < 0.5), slot, 0).astype(jnp.float32)
        y.append(mm(ones(spread), x))
    number = iota((rows, LANES), 0)
    pick = jnp.where(lax.rem(number // 4, 2) == 0, y[0], y[1])
    pick = jnp.where(iota((rows, LANES), 1) // segs == lax.rem(sender(number), blocks), pick, 0.0)
    held = jnp.sum(pick, axis=1, keepdims=True).astype(jnp.int32)

    own = row_of(holder, me // blocks)
    hot = ones(iota((n, LANES), 0) == own)
    rank = jnp.sum(hot * mm(hot, tri), axis=0, keepdims=True)
    away = lax.rem(own - me + n, n)
    block = lax.rem(away, 2) * (n // 2) + away // 2
    value = (block.astype(jnp.float32) * 2 + rank) * SEGMAX
    diag = iota((segs, LANES), 1) == lax.rem(me, blocks) * segs + iota((segs, LANES), 0)
    value = jnp.sum(jnp.where(diag, value, 0.0), axis=1, keepdims=True)
    size = sizes.astype(jnp.float32)
    square = iota((segs, segs), 1) == iota((segs, segs), 0)
    wide = jnp.where(square, size, 0.0)
    size = jnp.sum(wide, axis=1, keepdims=True)
    start = jnp.sum(
        jnp.where(
            iota((segs, segs), 1) < iota((segs, segs), 0), sizes.astype(jnp.float32), 0.0
        ),
        axis=1,
        keepdims=True,
    )
    r = iota((segs, reqs), 1).astype(jnp.float32)
    inside = (r >= start) & (r < start + size)
    place = jnp.sum(jnp.where(inside, value - start + r, 0.0), axis=0, keepdims=True)
    return place.astype(jnp.int32), held


def by_heads(x, rows, heads):
    return jnp.concatenate(
        [x[:, h * 8 : (h + 1) * 8, :].reshape(rows, LANES) for h in range(heads)], axis=1
    )


def main_kernel(
    n, tps,
    table, lens, q_in, source_in, wanted_in, sizes_in, holder_in, slot_in,
    resident, swap, down_in, up_in,
    mixed, delta_ref, arrived,
    q_ref, source, wanted, sizes, holder, slot, out_ref, ret,
    space, store, near_up, near_down, next_up, next_down, on_up, on_down, third_up, third_down,
    fourth, crossing, arr, qs, att, down, up, send, got, back, part, parts, plan, book,
    load, s1, r1, s2, r2, s3, r3, s4, r4, sx, rx, ss, rs, sb, rb, st, rt,
):
    reqs, width = q_ref.shape
    heads = width // HD
    pool, page = resident.shape[0], resident.shape[1]
    maxp = table.shape[0]
    news = arr.shape[0]
    pages = store.shape[0]
    slots, rank = down.shape[0], down.shape[1]
    rows = n * 8
    me, tp = lax.axis_index("req"), lax.axis_index("tp")
    zi, xi = me // RX, lax.rem(me, RX)
    above = lax.rem(zi + 1, RZ) * RX + xi
    below = lax.rem(zi + RZ - 1, RZ) * RX + xi
    barrier = pltpu.get_barrier_semaphore()

    loads = [
        pltpu.make_async_copy(swap, store, load.at[0]),
        pltpu.make_async_copy(resident, space.at[pl.ds(0, pool)], load.at[1]),
        pltpu.make_async_copy(down_in, down, load.at[2]),
        pltpu.make_async_copy(up_in, up, load.at[3]),
    ]
    small = [
        pltpu.make_async_copy(a, b, load.at[4 + i])
        for i, (a, b) in enumerate(
            (
                (source_in, source),
                (wanted_in, wanted),
                (sizes_in, sizes),
                (holder_in, holder),
                (slot_in, slot),
                (q_in, q_ref),
            )
        )
    ]
    loads[0].start()
    for copy in small:
        copy.start()

    def hello(d, c):
        pl.semaphore_signal(
            barrier, inc=1, device_id={"req": lax.rem(me + d, n)}, device_id_type=MESH
        )
        return c

    lax.fori_loop(1, n, hello, 0)
    for d in range(1, tps):
        pl.semaphore_signal(
            barrier, inc=1, device_id={"tp": lax.rem(tp + d, tps)}, device_id_type=MESH
        )
    loads[0].wait()
    pl.semaphore_wait(barrier, n - 1 + tps - 1)

    def hop(src, dst, ssem, rsem, to):
        return pltpu.make_async_remote_copy(
            src_ref=src, dst_ref=dst, send_sem=ssem, recv_sem=rsem,
            device_id={"req": to}, device_id_type=MESH,
        )

    sides = (above, below)
    near, nxt, on, third = (
        (near_up, near_down), (next_up, next_down), (on_up, on_down), (third_up, third_down)
    )

    def part_of(ref, c):
        return ref.at[pl.ds(c * CHUNK, CHUNK)]

    first, second, later, last = [], [], [], []
    for c in range(pages // CHUNK):
        for w in range(2):
            first.append(
                hop(part_of(store, c), part_of(near[w], c), s1.at[w, c], r1.at[w, c], sides[w])
            )
            second.append(
                hop(part_of(near[w], c), part_of(nxt[w], c), s2.at[w, c], r2.at[w, c], sides[w])
            )
    for c in range(NEAR // CHUNK):
        for w in range(2):
            later.append(
                hop(part_of(on[w], c), part_of(third[w], c), s3.at[w, c], r3.at[w, c], sides[w])
            )
    for w in range(2):
        last.append(
            hop(third[w].at[pl.ds(0, FAR)], part_of(fourth, w), s4.at[w], r4.at[w], sides[w])
        )
    for copy in first:
        copy.start()
    for copy in loads[1:]:
        copy.start()

    for copy in small:
        copy.wait()
    plan[...] = ring_plan(source[...], wanted[...], zi, xi, n, pages, news)
    enter = pltpu.make_async_copy(plan, book, load.at[0])
    enter.start()
    slot_place, hs = chain_plan(n, reqs, sizes[...], holder[...], slot[...], me)
    put = ones(iota((rows, reqs), 0) == slot_place).astype(jnp.bfloat16)
    qs[...] = jnp.zeros_like(qs)
    for h in range(heads):
        qs[pl.ds(h, reqs, stride=8), :] = q_ref[:, h * HD : (h + 1) * HD].astype(jnp.float32)
    enter.wait()

    def within(i, ref):
        return jnp.clip(i, 0, ref.shape[0] - 1)

    def land(z, x):
        return pool + (z * RX + x) * CAP

    def cross_copy(k, dx):
        z = lax.rem(zi + RZ - k, RZ)
        return hop(
            crossing.at[k, dx - 1], space.at[pl.ds(land(z, xi), CAP)],
            sx.at[k, dx - 1], rx.at[k, dx - 1], z_row(dx),
        )

    def z_row(dx):
        return zi * RX + lax.rem(xi + dx, RX)

    def cross(k, ref):
        z = lax.rem(zi + RZ - k, RZ)
        for dx in (2, 1, 3):
            xd = lax.rem(xi + dx, RX)
            for r in range(CAP):
                crossing[k, dx - 1, r] = ref[within(book[z, xd * CAP + r], ref)]
            cross_copy(k, dx).start()
        for r in range(CAP):
            space[land(z, xi) + r] = ref[within(book[z, xi * CAP + r], ref)]

    cross(0, store)
    for a, b in zip(first, second):
        a.wait_recv()
        b.start()
    cross(1, near_up)
    cross(7, near_down)
    for copy in second:
        copy.wait_recv()
    for w in range(2):
        for c in range(NEAR // CHUNK):
            for i in range(CHUNK):
                on[w][c * CHUNK + i] = nxt[w][within(book[16 + c * CHUNK + i, w], nxt[w])]
            later[c * 2 + w].start()
    cross(2, next_up)
    cross(6, next_down)
    for i, copy in enumerate(later):
        copy.wait_recv()
        if i < 2:
            last[i].start()
    cross(3, third_up)
    cross(5, third_down)
    for copy in last:
        copy.wait_recv()
    cross(4, fourth)
    for copy in loads[1:]:
        copy.wait()
    for copy in first + second + later + last:
        copy.wait_send()
    for k in range(RZ):
        for dx in range(1, RX):
            cross_copy(k, dx).wait_send()
            z = lax.rem(zi + RZ - k, RZ)
            x = lax.rem(xi + RX - dx, RX)
            hop(
                crossing.at[k, dx - 1], space.at[pl.ds(land(z, x), CAP)],
                sx.at[k, dx - 1], rx.at[k, dx - 1], z_row(dx),
            ).wait_recv()

    def spot(j):
        return pool + jnp.clip(book[8 + xi // 2, lax.rem(xi, 2) * news + j], 0, n * CAP - 1)

    def pick(j, c):
        arr[j] = space[spot(j)]
        return c

    lax.fori_loop(0, news, pick, 0)
    keep = pltpu.make_async_copy(arr, arrived, load.at[0])
    keep.start()

    step = 8

    def page_at(r, k):
        t = table[k, r]
        return jnp.where(t < pool, jnp.clip(t, 0, pool - 1), spot(jnp.clip(t - pool, 0, news - 1)))

    def body(b, c):
        scores, spots = [], []
        for i in range(step):
            r = b * step + i
            at = [page_at(r, k) for k in range(maxp)]
            keys = jnp.concatenate([space[a, :, :HD] for a in at], axis=0)
            q = qs[pl.ds(pl.multiple_of(r * 8, 8), 8), :].astype(jnp.bfloat16)
            s = lax.dot_general(
                q, keys, (((1,), (1,)), ((), ())), preferred_element_type=jnp.float32
            ) * (HD ** (-0.5))
            pos = lax.broadcasted_iota(jnp.int32, s.shape, 1)
            scores.append(jnp.where(pos < lens[r], s, NEG))
            spots.append(at)
        s = jnp.concatenate(scores, axis=0)
        e = jnp.exp(s - jnp.max(s, axis=1, keepdims=True))
        p = e / jnp.sum(e, axis=1, keepdims=True)
        for i in range(step):
            vals = jnp.concatenate([space[a, :, HD:] for a in spots[i]], axis=0)
            o = jnp.dot(
                p[i * 8 : (i + 1) * 8].astype(jnp.bfloat16),
                vals,
                preferred_element_type=jnp.float32,
            )
            att[pl.ds(pl.multiple_of((b * step + i) * 8, 8), 8), :] = o
        return c

    lax.fori_loop(0, reqs // step, body, 0)
    for h in range(heads):
        out_ref[:, h * HD : (h + 1) * HD] = att[pl.ds(h, reqs, stride=8), :].astype(jnp.bfloat16)

    keep_mixed = pltpu.make_async_copy(out_ref, mixed, load.at[1])
    keep_mixed.start()
    g = jnp.dot(put, out_ref[...], preferred_element_type=jnp.float32)
    zero = jnp.zeros((8, LANES), jnp.float32)
    groups = 2
    blocks = n // groups
    group_rows = blocks * 8

    def there(p):
        to = lax.rem(me + apart(p, n), n)
        return hop(send.at[p], got.at[p], ss.at[p], rs.at[p], to)

    def home(p):
        to = lax.rem(me - apart(p, n) + n, n)
        return hop(ret.at[p], back.at[p], sb.at[p], rb.at[p], to)

    def each(group, act):
        def one(p, c):
            act(p)
            return c

        lax.fori_loop(max(1, group * blocks), (group + 1) * blocks, one, 0)

    for group in range(groups):
        for p in range(group * blocks, (group + 1) * blocks):
            block = [g[p * 8 : (p + 1) * 8, h * HD : (h + 1) * HD] for h in range(heads)]
            block += [zero] * (8 - heads)
            send[p] = jnp.concatenate(block, axis=0).astype(jnp.bfloat16)
        each(group, lambda p: there(p).start())
    got[0] = send[0]

    lane = iota((group_rows, LANES), 1)
    per = LANES // rank
    half = group_rows // 2
    low = iota((half, LANES), 1) < rank
    exchange = []
    for group in range(groups):
        exchange.append(
            [
                pltpu.make_async_remote_copy(
                    src_ref=part.at[group], dst_ref=parts.at[group, d - 1],
                    send_sem=st.at[group, d - 1], recv_sem=rt.at[group, d - 1],
                    device_id={"tp": lax.rem(tp + d, tps)}, device_id_type=MESH,
                )
                for d in range(1, tps)
            ]
        )
    held = []
    for group in range(groups):
        each(group, lambda p: there(p).wait_recv())
        mine = slice(group * blocks, (group + 1) * blocks)
        a = by_heads(got[mine].astype(jnp.float32), group_rows, heads).astype(jnp.bfloat16)
        held.append(hs[group * group_rows : (group + 1) * group_rows])
        total = jnp.zeros((group_rows, LANES), jnp.float32)
        for c in range(0, slots, 2 * per):
            w = down[c : c + 2 * per].reshape(2 * per * rank, width)
            s = mmt(a, w)
            total = total + jnp.where(held[group] == c + lane // rank, s[:, :LANES], 0.0)
            total = total + jnp.where(held[group] == c + per + lane // rank, s[:, LANES:], 0.0)
        total = total + pltpu.roll(total, rank, 1)
        part[group] = jnp.where(low, total[:half], total[half:])
        for copy in exchange[group]:
            copy.start()
    for group in range(groups):
        for copy in exchange[group]:
            copy.wait_recv()
        acc = part[group]
        for d in range(tps - 1):
            acc = acc + parts[group, d]
        turned = pltpu.roll(acc, rank, 1)
        shrunk = jnp.concatenate(
            [jnp.where(low, acc, turned), jnp.where(low, turned, acc)], axis=0
        ).astype(jnp.bfloat16)
        spread = jnp.concatenate(
            [
                jnp.where(held[group] == c + lane // rank, shrunk, jnp.zeros((), jnp.bfloat16))
                for c in range(0, slots, per)
            ],
            axis=1,
        )
        t = mm(spread, up[...].reshape(slots * rank, width)) * low_rank_scale
        for p in range(blocks):
            block = [t[p * 8 : (p + 1) * 8, h * HD : (h + 1) * HD] for h in range(heads)]
            block += [zero] * (8 - heads)
            ret[group * blocks + p] = jnp.concatenate(block, axis=0).astype(jnp.bfloat16)
        each(group, lambda p: home(p).start())
    back[0] = ret[0]
    for group in range(groups):
        each(group, lambda p: there(p).wait_send())
        for copy in exchange[group]:
            copy.wait_send()
    keep.wait()
    keep_mixed.wait()
    for group in range(groups):
        each(group, lambda p: home(p).wait_recv())
    b = by_heads(back[...].astype(jnp.float32), rows, heads).astype(jnp.bfloat16)
    delta_ref[...] = lax.dot_general(
        put, b, (((0,), (0,)), ((), ())), preferred_element_type=jnp.float32
    ).astype(jnp.bfloat16)
    for group in range(groups):
        each(group, lambda p: home(p).wait_send())


def leave_kernel(count, parts, *refs):
    ins, outs, held, sems = refs[:count], refs[count : 2 * count], refs[2 * count : 3 * count], refs[-1]
    into, out = [], []
    for i in range(count):
        rows = ins[i].shape[0] // parts[i]
        for c in range(parts[i]):
            span = pl.ds(c * rows, rows)
            at = len(into)
            into.append(pltpu.make_async_copy(ins[i].at[span], held[i].at[span], sems.at[0, at]))
            out.append(pltpu.make_async_copy(held[i].at[span], outs[i].at[span], sems.at[1, at]))
    for copy in into:
        copy.start()
    for a, b in zip(into, out):
        a.wait()
        b.start()
    for copy in out:
        copy.wait()


def leave(*arrays):
    count = len(arrays)
    parts = [8 if a.ndim == 3 else 1 for a in arrays]
    hbm = pl.BlockSpec(memory_space=pl.ANY)
    return pl.pallas_call(
        functools.partial(leave_kernel, count, parts),
        out_shape=tuple(jax.ShapeDtypeStruct(a.shape, a.dtype) for a in arrays),
        in_specs=[hbm] * count,
        out_specs=(hbm,) * count,
        scratch_shapes=[pltpu.VMEM(a.shape, a.dtype) for a in arrays]
        + [pltpu.SemaphoreType.DMA((2, sum(parts)))],
        name="leave",
    )(*arrays)


def serve(n, tps, table, lens, queries, source, wanted, sizes, holder, slot, resident, swap, down, up):
    reqs, width = queries.shape
    pool, page, kvw = resident.shape
    news = source.size // n
    rows = n * 8
    smem = pl.BlockSpec(memory_space=pltpu.SMEM)
    vmem = pl.BlockSpec(memory_space=pltpu.VMEM)
    hbm = pl.BlockSpec(memory_space=pl.ANY)
    dma = pltpu.SemaphoreType.DMA
    bf16, f32 = jnp.bfloat16, jnp.float32
    stores = swap.shape[0]

    def held(count):
        return pltpu.VMEM((count, page, kvw), bf16)

    return pl.pallas_call(
        functools.partial(main_kernel, n, tps),
        out_shape=(
            jax.ShapeDtypeStruct((reqs, width), bf16),
            jax.ShapeDtypeStruct((reqs, width), bf16),
            jax.ShapeDtypeStruct((news, page, kvw), bf16),
        ),
        in_specs=[smem] * 2 + [hbm] * 10,
        out_specs=(hbm, vmem, hbm),
        scratch_shapes=[
            pltpu.VMEM(queries.shape, bf16),
            pltpu.VMEM(source.shape, jnp.int32),
            pltpu.VMEM(wanted.shape, jnp.int32),
            pltpu.VMEM(sizes.shape, jnp.int32),
            pltpu.VMEM(holder.shape, jnp.int32),
            pltpu.VMEM(slot.shape, jnp.int32),
            pltpu.VMEM(queries.shape, bf16),
            pltpu.VMEM((n, 64, LANES), bf16),
            held(pool + n * CAP),
            held(stores), held(stores), held(stores), held(stores), held(stores),
            held(NEAR), held(NEAR), held(NEAR), held(NEAR), held(2 * FAR),
            pltpu.VMEM((RZ, RX - 1, CAP, page, kvw), bf16),
            held(news),
            pltpu.VMEM((reqs * 8, LANES), f32),
            pltpu.VMEM((reqs * 8, LANES), f32),
            pltpu.VMEM(down.shape, bf16),
            pltpu.VMEM(up.shape, bf16),
            pltpu.VMEM((n, 64, LANES), bf16),
            pltpu.VMEM((n, 64, LANES), bf16),
            pltpu.VMEM((n, 64, LANES), bf16),
            pltpu.VMEM((2, rows // 4, LANES), f32),
            pltpu.VMEM((2, tps - 1, rows // 4, LANES), f32),
            pltpu.VMEM((16 + stores, LANES), jnp.int32),
            pltpu.SMEM((16 + stores, LANES), jnp.int32),
            dma((10,)),
            dma((2, stores // CHUNK)), dma((2, stores // CHUNK)),
            dma((2, stores // CHUNK)), dma((2, stores // CHUNK)),
            dma((2, NEAR // CHUNK)), dma((2, NEAR // CHUNK)), dma((2,)), dma((2,)),
            dma((RZ, RX - 1)), dma((RZ, RX - 1)),
            dma((n,)), dma((n,)), dma((n,)), dma((n,)),
            dma((2, tps - 1)), dma((2, tps - 1)),
        ],
        compiler_params=pltpu.CompilerParams(
            collective_id=0, has_side_effects=True, vmem_limit_bytes=56 << 20
        ),
        name="serve",
    )(table, lens, queries, source, wanted, sizes, holder, slot, resident, swap, down, up)


def local(
    queries,
    resident_kv,
    swap_kv,
    page_table,
    lengths,
    resume_source,
    resume_page,
    seg_lengths,
    segment_adapter_holder,
    seg_slot,
    adapter_down,
    adapter_up,
):
    results = serve(
        lax.axis_size("req"),
        lax.axis_size("tp"),
        page_table.T,
        lengths,
        queries,
        resume_source.reshape(-1, LANES),
        resume_page.reshape(-1, LANES),
        seg_lengths,
        segment_adapter_holder.reshape(-1, LANES),
        seg_slot.reshape(-1, LANES),
        resident_kv,
        swap_kv,
        adapter_down,
        adapter_up,
    )
    mixed, delta, arrived = results
    return leave(mixed, delta, arrived)


def solution(mesh):
    return jax.shard_map(
        local,
        mesh=mesh,
        in_specs=(
            P("req", "tp"),
            P("req", None, "tp"),
            P("req", None, "tp"),
            P("req", None),
            P("req"),
            P(),
            P(),
            P("req", None),
            P(),
            P(),
            P("req", None, "tp"),
            P("req", None, "tp"),
        ),
        out_specs=(P("req", "tp"), P("req", "tp"), P("req", None, "tp")),
        check_vma=False,
    )
```

```python
import functools

import jax
import jax.numpy as jnp
from jax import lax
from jax.experimental import pallas as pl
from jax.experimental.pallas import tpu as pltpu
from jax.sharding import PartitionSpec as P

HD = 128
SEGMAX = 4
LANES = 128
MESH = pl.DeviceIdType.MESH
NEG = -1e30
RZ, RX = 8, 4
CAP = 4
CHUNK = 8
NEAR = 24
FAR = 8
GROUPS = 4

low_rank_scale = 2.0


def iota(shape, dim):
    return lax.broadcasted_iota(jnp.int32, shape, dim)


def ones(mask):
    return jnp.where(mask, 1.0, 0.0)


def mm(a, b):
    return jnp.dot(
        a.astype(jnp.bfloat16), b.astype(jnp.bfloat16), preferred_element_type=jnp.float32
    )


def mmt(a, b):
    return lax.dot_general(
        a.astype(jnp.bfloat16),
        b.astype(jnp.bfloat16),
        (((1,), (1,)), ((), ())),
        preferred_element_type=jnp.float32,
    )


def before(n, block):
    r, c = iota((n, n), 0), iota((n, n), 1)
    return ones((r < c) & (r // block == c // block))


def row_of(x, i):
    return jnp.sum(jnp.where(iota(x.shape, 0) == i, x, jnp.zeros((), x.dtype)), axis=0, keepdims=True)


def ring_plan(source, wanted, zi, xi, stores, pages, per_block):
    shape = (RZ, pages)
    zs = iota(shape, 0)
    need, need_even = [], []
    for zd in range(RZ):
        total = jnp.zeros(shape, jnp.float32)
        even = jnp.zeros(shape, jnp.float32)
        for h in range(2):
            s = source[2 * zd + h : 2 * zd + h + 1]
            w = wanted[2 * zd + h : 2 * zd + h + 1]
            a = ones(iota((RZ, LANES), 0) * RX + xi == s)
            b = ones(iota((pages, LANES), 0) == w)
            total = total + mmt(a, b)
            x = 2 * h + iota((RZ, LANES), 1) // per_block
            even = even + mmt(a * ones(lax.rem(x - xi + RX, 2) == 0), b)
        need.append(total)
        need_even.append(even)

    def wants(needed, k):
        found = jnp.zeros(shape, jnp.float32)
        for zd in range(RZ):
            found = jnp.where(lax.rem(zd - zs + RZ, RZ) == k, needed[zd], found)
        return ones(found > 0.5)

    at = {k: wants(need, k) for k in (3, 4, 5)}
    at_even = {k: wants(need_even, k) for k in (3, 5)}
    tri = before(pages, pages)
    far = at[4]
    far_up = far * ones(mm(far, tri) < FAR - 0.5)
    far_down = far - far_up
    lists = {}
    for name, f4, k in (("up", far_up, 3), ("down", far_down, 5)):
        f3 = at[k] * (1.0 - f4)
        half = at_even[k] * f3
        other = f3 - half
        place4 = mm(f4, tri)
        place3 = half * (FAR + mm(half, tri)) + other * (NEAR - CHUNK + mm(other, tri))
        lists[name] = (f4, f3, place4, f4 * place4 + place3)
    page_id = iota(shape, 1).astype(jnp.float32)
    k = lax.rem(zi - zs + RZ, RZ)
    spot4 = jnp.where(far_up > 0.5, lists["up"][2], FAR + lists["down"][2])
    spot = jnp.where(
        k == 3, lists["up"][3], jnp.where(k == 5, lists["down"][3], jnp.where(k == 4, spot4, page_id))
    )
    send = []
    for name, owner in (("up", lax.rem(zi + RZ - 2, RZ)), ("down", lax.rem(zi + 2, RZ))):
        f4, f3, _, place = lists[name]
        used = row_of(f4 + f3, owner)
        p = row_of(place, owner)
        hit = (iota((pages, pages), 0).astype(jnp.float32) == p) & (used > 0.5)
        send.append(
            jnp.sum(
                jnp.where(hit, iota((pages, pages), 1).astype(jnp.float32), 0.0), axis=1, keepdims=True
            )
        )
    tri2 = before(LANES, per_block)
    table = jnp.zeros((RZ, LANES), jnp.float32)
    landing = []
    lane = iota((1, LANES), 1)
    for h in range(2):
        s = row_of(source, 2 * zi + h)
        w = row_of(wanted, 2 * zi + h)
        hot = ones(iota((stores, LANES), 0) == s)
        rank = jnp.sum(hot * mm(hot, tri2), axis=0, keepdims=True)
        landing.append(s.astype(jnp.float32) * CAP + rank)
        v = mm(spot, ones(iota((pages, LANES), 0) == w))
        v = v * ones(iota((RZ, LANES), 0) * RX + xi == s)
        column = (2 * h + lane // per_block) * CAP + rank.astype(jnp.int32)
        table = table + mmt(v, ones(iota((LANES, LANES), 0) == column))
    top = jnp.concatenate(
        [table, landing[0], landing[1], jnp.zeros((RZ - 2, LANES), jnp.float32)], axis=0
    )
    wide = iota((pages, LANES), 1)
    tail = jnp.where(wide == 0, send[0], jnp.where(wide == 1, send[1], 0.0))
    return jnp.concatenate([top, tail], axis=0).astype(jnp.int32)


def apart(p, n):
    return GROUPS * lax.rem(p, n // GROUPS) + p // (n // GROUPS)


def chain_plan(n, reqs, sizes, holder, slot, me):
    segs = sizes.shape[1]
    rows = n * 8
    blocks = LANES // segs
    tri = before(LANES, segs)
    mine = ones(holder == me)
    order = mm(mine, tri)

    def sender(number):
        return lax.rem(me - apart(number // 8, n) + n, n)

    wide = (rows, holder.shape[0])
    spread = sender(iota(wide, 0)) // blocks == iota(wide, 1)
    y = []
    for q in range(2):
        x = jnp.where((mine > 0.5) & (jnp.abs(order - q) < 0.5), slot, 0).astype(jnp.float32)
        y.append(mm(ones(spread), x))
    number = iota((rows, LANES), 0)
    pick = jnp.where(lax.rem(number // 4, 2) == 0, y[0], y[1])
    pick = jnp.where(iota((rows, LANES), 1) // segs == lax.rem(sender(number), blocks), pick, 0.0)
    held = jnp.sum(pick, axis=1, keepdims=True).astype(jnp.int32)

    own = row_of(holder, me // blocks)
    hot = ones(iota((n, LANES), 0) == own)
    rank = jnp.sum(hot * mm(hot, tri), axis=0, keepdims=True)
    away = lax.rem(own - me + n, n)
    block = lax.rem(away, GROUPS) * (n // GROUPS) + away // GROUPS
    value = (block.astype(jnp.float32) * 2 + rank) * SEGMAX
    diag = iota((segs, LANES), 1) == lax.rem(me, blocks) * segs + iota((segs, LANES), 0)
    value = jnp.sum(jnp.where(diag, value, 0.0), axis=1, keepdims=True)
    size = sizes.astype(jnp.float32)
    square = iota((segs, segs), 1) == iota((segs, segs), 0)
    wide = jnp.where(square, size, 0.0)
    size = jnp.sum(wide, axis=1, keepdims=True)
    start = jnp.sum(
        jnp.where(
            iota((segs, segs), 1) < iota((segs, segs), 0), sizes.astype(jnp.float32), 0.0
        ),
        axis=1,
        keepdims=True,
    )
    r = iota((segs, reqs), 1).astype(jnp.float32)
    inside = (r >= start) & (r < start + size)
    place = jnp.sum(jnp.where(inside, value - start + r, 0.0), axis=0, keepdims=True)
    return place.astype(jnp.int32), held


def by_heads(x, rows, heads):
    return jnp.concatenate(
        [x[:, h * 8 : (h + 1) * 8, :].reshape(rows, LANES) for h in range(heads)], axis=1
    )


def main_kernel(
    n, tps,
    table, lens, q_in, source_in, wanted_in, sizes_in, holder_in, slot_in,
    resident, swap, down_in, up_in,
    mixed, delta_ref, arrived,
    q_ref, source, wanted, sizes, holder, slot, out_ref, ret,
    space, store, near_up, near_down, next_up, next_down, on_up, on_down, third_up, third_down,
    rest_up, rest_down, all_up, all_down,
    fourth, crossing, arr, qs, att, down, up, send, got, back, part, parts, plan, book,
    load, s1, r1, s2, r2, s3, r3, s4, r4, sx, rx, ss, rs, sb, rb, st, rt,
):
    reqs, width = q_ref.shape
    heads = width // HD
    pool, page = resident.shape[0], resident.shape[1]
    maxp = table.shape[0]
    news = arr.shape[0]
    pages = store.shape[0]
    slots, rank = down.shape[0], down.shape[1]
    rows = n * 8
    me, tp = lax.axis_index("req"), lax.axis_index("tp")
    zi, xi = me // RX, lax.rem(me, RX)
    above = lax.rem(zi + 1, RZ) * RX + xi
    below = lax.rem(zi + RZ - 1, RZ) * RX + xi
    barrier = pltpu.get_barrier_semaphore()

    loads = [
        pltpu.make_async_copy(swap, store, load.at[0]),
        pltpu.make_async_copy(resident, space.at[pl.ds(0, pool)], load.at[1]),
        pltpu.make_async_copy(down_in, down, load.at[2]),
        pltpu.make_async_copy(up_in, up, load.at[3]),
    ]
    small = [
        pltpu.make_async_copy(a, b, load.at[4 + i])
        for i, (a, b) in enumerate(
            (
                (source_in, source),
                (wanted_in, wanted),
                (sizes_in, sizes),
                (holder_in, holder),
                (slot_in, slot),
                (q_in, q_ref),
            )
        )
    ]
    loads[0].start()
    for copy in small:
        copy.start()

    def hello(d, c):
        pl.semaphore_signal(
            barrier, inc=1, device_id={"req": lax.rem(me + d, n)}, device_id_type=MESH
        )
        return c

    lax.fori_loop(1, n, hello, 0)
    for d in range(1, tps):
        pl.semaphore_signal(
            barrier, inc=1, device_id={"tp": lax.rem(tp + d, tps)}, device_id_type=MESH
        )
    loads[0].wait()
    pl.semaphore_wait(barrier, n - 1 + tps - 1)

    def hop(src, dst, ssem, rsem, to):
        return pltpu.make_async_remote_copy(
            src_ref=src, dst_ref=dst, send_sem=ssem, recv_sem=rsem,
            device_id={"req": to}, device_id_type=MESH,
        )

    sides = (above, below)
    near, nxt, on, third = (
        (near_up, near_down), (next_up, next_down), (on_up, on_down), (third_up, third_down)
    )
    rest, whole = (rest_up, rest_down), (all_up, all_down)
    early = NEAR // CHUNK - 1

    def part_of(ref, c):
        return ref.at[pl.ds(c * CHUNK, CHUNK)]

    first, second, later, last = [], [], [], []
    for c in range(pages // CHUNK):
        for w in range(2):
            first.append(
                hop(part_of(store, c), part_of(near[w], c), s1.at[w, c], r1.at[w, c], sides[w])
            )
            second.append(
                hop(part_of(near[w], c), part_of(nxt[w], c), s2.at[w, c], r2.at[w, c], sides[w])
            )
    for c in range(NEAR // CHUNK):
        for w in range(2):
            to = part_of(third[w], c) if c < early else rest[w]
            later.append(hop(part_of(on[w], c), to, s3.at[w, c], r3.at[w, c], sides[w]))
    for w in range(2):
        last.append(
            hop(third[w].at[pl.ds(0, FAR)], part_of(fourth, w), s4.at[w], r4.at[w], sides[w])
        )
    for copy in first:
        copy.start()
    for copy in loads[1:]:
        copy.start()

    for copy in small:
        copy.wait()
    plan[...] = ring_plan(source[...], wanted[...], zi, xi, n, pages, news)
    enter = pltpu.make_async_copy(plan, book, load.at[0])
    enter.start()
    slot_place, hs = chain_plan(n, reqs, sizes[...], holder[...], slot[...], me)
    put = ones(iota((rows, reqs), 0) == slot_place).astype(jnp.bfloat16)
    qs[...] = jnp.zeros_like(qs)
    for h in range(heads):
        qs[pl.ds(h, reqs, stride=8), :] = q_ref[:, h * HD : (h + 1) * HD].astype(jnp.float32)
    enter.wait()

    def within(i, ref):
        return jnp.clip(i, 0, ref.shape[0] - 1)

    def land(z, x):
        return pool + (z * RX + x) * CAP

    def cross_copy(k, dx):
        z = lax.rem(zi + RZ - k, RZ)
        return hop(
            crossing.at[k, dx - 1], space.at[pl.ds(land(z, xi), CAP)],
            sx.at[k, dx - 1], rx.at[k, dx - 1], z_row(dx),
        )

    def z_row(dx):
        return zi * RX + lax.rem(xi + dx, RX)

    def cross(k, ref, ways=(2, 1, 3, 0)):
        z = lax.rem(zi + RZ - k, RZ)
        for dx in ways:
            if dx == 0:
                for r in range(CAP):
                    space[land(z, xi) + r] = ref[within(book[z, xi * CAP + r], ref)]
                continue
            xd = lax.rem(xi + dx, RX)
            for r in range(CAP):
                crossing[k, dx - 1, r] = ref[within(book[z, xd * CAP + r], ref)]
            cross_copy(k, dx).start()

    cross(0, store)
    for a, b in zip(first, second):
        a.wait_recv()
        b.start()
    cross(1, near_up)
    cross(7, near_down)
    for copy in second:
        copy.wait_recv()
    for w in range(2):
        for c in range(NEAR // CHUNK):
            for i in range(CHUNK):
                on[w][c * CHUNK + i] = nxt[w][within(book[16 + c * CHUNK + i, w], nxt[w])]
            later[c * 2 + w].start()
    cross(2, next_up)
    cross(6, next_down)
    for i, copy in enumerate(later[: 2 * early]):
        copy.wait_recv()
        if i < 2:
            last[i].start()
    cross(3, third_up, (2, 0))
    cross(5, third_down, (2, 0))
    for w in range(2):
        whole[w][pl.ds(0, early * CHUNK)] = third[w][...]
    for copy in later[2 * early :]:
        copy.wait_recv()
    for w in range(2):
        whole[w][pl.ds(early * CHUNK, CHUNK)] = rest[w][...]
    cross(3, all_up, (1, 3))
    cross(5, all_down, (1, 3))
    for copy in last:
        copy.wait_recv()
    cross(4, fourth)
    for copy in loads[1:]:
        copy.wait()
    for k in range(RZ):
        for dx in range(1, RX):
            z = lax.rem(zi + RZ - k, RZ)
            x = lax.rem(xi + RX - dx, RX)
            hop(
                crossing.at[k, dx - 1], space.at[pl.ds(land(z, x), CAP)],
                sx.at[k, dx - 1], rx.at[k, dx - 1], z_row(dx),
            ).wait_recv()

    def spot(j):
        return pool + jnp.clip(book[8 + xi // 2, lax.rem(xi, 2) * news + j], 0, n * CAP - 1)

    step = 16

    def page_at(r, k):
        t = table[k, r]
        return jnp.where(t < pool, jnp.clip(t, 0, pool - 1), spot(jnp.clip(t - pool, 0, news - 1)))

    def body(b, c):
        scores, spots = [], []
        for i in range(step):
            r = b * step + i
            at = [page_at(r, k) for k in range(maxp)]
            keys = jnp.concatenate([space[a, :, :HD] for a in at], axis=0)
            q = qs[pl.ds(pl.multiple_of(r * 8, 8), 8), :].astype(jnp.bfloat16)
            s = lax.dot_general(
                q, keys, (((1,), (1,)), ((), ())), preferred_element_type=jnp.float32
            ) * (HD ** (-0.5))
            pos = lax.broadcasted_iota(jnp.int32, s.shape, 1)
            scores.append(jnp.where(pos < lens[r], s, NEG))
            spots.append(at)
        s = jnp.concatenate(scores, axis=0)
        e = jnp.exp(s - jnp.max(s, axis=1, keepdims=True))
        p = e / jnp.sum(e, axis=1, keepdims=True)
        for i in range(step):
            vals = jnp.concatenate([space[a, :, HD:] for a in spots[i]], axis=0)
            o = jnp.dot(
                p[i * 8 : (i + 1) * 8].astype(jnp.bfloat16),
                vals,
                preferred_element_type=jnp.float32,
            )
            att[pl.ds(pl.multiple_of((b * step + i) * 8, 8), 8), :] = o
        return c

    lax.fori_loop(0, reqs // step, body, 0)
    for h in range(heads):
        out_ref[:, h * HD : (h + 1) * HD] = att[pl.ds(h, reqs, stride=8), :].astype(jnp.bfloat16)

    keep_mixed = pltpu.make_async_copy(out_ref, mixed, load.at[1])
    keep_mixed.start()
    g = jnp.dot(put, out_ref[...], preferred_element_type=jnp.float32)
    zero = jnp.zeros((8, LANES), jnp.float32)
    groups = GROUPS
    blocks = n // groups
    group_rows = blocks * 8

    def there(p):
        to = lax.rem(me + apart(p, n), n)
        return hop(send.at[p], got.at[p], ss.at[p], rs.at[p], to)

    def home(p):
        to = lax.rem(me - apart(p, n) + n, n)
        return hop(ret.at[p], back.at[p], sb.at[p], rb.at[p], to)

    def each(group, act):
        def one(p, c):
            act(p)
            return c

        lax.fori_loop(max(1, group * blocks), (group + 1) * blocks, one, 0)

    for group in range(groups):
        for p in range(group * blocks, (group + 1) * blocks):
            block = [g[p * 8 : (p + 1) * 8, h * HD : (h + 1) * HD] for h in range(heads)]
            block += [zero] * (8 - heads)
            send[p] = jnp.concatenate(block, axis=0).astype(jnp.bfloat16)
        each(group, lambda p: there(p).start())
    got[0] = send[0]

    lane = iota((group_rows, LANES), 1)
    per = LANES // rank
    half = group_rows // 2
    low = iota((half, LANES), 1) < rank
    exchange = []
    for group in range(groups):
        exchange.append(
            [
                pltpu.make_async_remote_copy(
                    src_ref=part.at[group], dst_ref=parts.at[group, d - 1],
                    send_sem=st.at[group, d - 1], recv_sem=rt.at[group, d - 1],
                    device_id={"tp": lax.rem(tp + d, tps)}, device_id_type=MESH,
                )
                for d in range(1, tps)
            ]
        )
    held = [hs[group * group_rows : (group + 1) * group_rows] for group in range(groups)]

    def shrink(group):
        each(group, lambda p: there(p).wait_recv())
        mine = slice(group * blocks, (group + 1) * blocks)
        a = by_heads(got[mine].astype(jnp.float32), group_rows, heads).astype(jnp.bfloat16)
        total = jnp.zeros((group_rows, LANES), jnp.float32)
        for c in range(0, slots, 2 * per):
            w = down[c : c + 2 * per].reshape(2 * per * rank, width)
            s = mmt(a, w)
            total = total + jnp.where(held[group] == c + lane // rank, s[:, :LANES], 0.0)
            total = total + jnp.where(held[group] == c + per + lane // rank, s[:, LANES:], 0.0)
        total = total + pltpu.roll(total, rank, 1)
        part[group] = jnp.where(low, total[:half], total[half:])
        for copy in exchange[group]:
            copy.start()

    def expand(group):
        for copy in exchange[group]:
            copy.wait_recv()
        acc = part[group]
        for d in range(tps - 1):
            acc = acc + parts[group, d]
        turned = pltpu.roll(acc, rank, 1)
        shrunk = jnp.concatenate(
            [jnp.where(low, acc, turned), jnp.where(low, turned, acc)], axis=0
        ).astype(jnp.bfloat16)
        spread = jnp.concatenate(
            [
                jnp.where(held[group] == c + lane // rank, shrunk, jnp.zeros((), jnp.bfloat16))
                for c in range(0, slots, per)
            ],
            axis=1,
        )
        t = mm(spread, up[...].reshape(slots * rank, width)) * low_rank_scale
        for p in range(blocks):
            block = [t[p * 8 : (p + 1) * 8, h * HD : (h + 1) * HD] for h in range(heads)]
            block += [zero] * (8 - heads)
            ret[group * blocks + p] = jnp.concatenate(block, axis=0).astype(jnp.bfloat16)
        each(group, lambda p: home(p).start())

    def pick(j, c):
        arr[j] = space[spot(j)]
        return c

    lax.fori_loop(0, news, pick, 0)
    keep = pltpu.make_async_copy(arr, arrived, load.at[0])
    keep.start()
    shrink(0)
    shrink(1)
    expand(0)
    shrink(2)
    expand(1)
    shrink(3)
    expand(2)
    expand(3)
    back[0] = ret[0]
    for group in range(groups):
        each(group, lambda p: there(p).wait_send())
        for copy in exchange[group]:
            copy.wait_send()
    for copy in first + second + later + last:
        copy.wait_send()
    for k in range(RZ):
        for dx in range(1, RX):
            cross_copy(k, dx).wait_send()
    keep.wait()
    keep_mixed.wait()
    for group in range(groups):
        each(group, lambda p: home(p).wait_recv())
    b = by_heads(back[...].astype(jnp.float32), rows, heads).astype(jnp.bfloat16)
    delta_ref[...] = lax.dot_general(
        put, b, (((0,), (0,)), ((), ())), preferred_element_type=jnp.float32
    ).astype(jnp.bfloat16)
    for group in range(groups):
        each(group, lambda p: home(p).wait_send())


def leave_kernel(count, parts, *refs):
    ins, outs, held, sems = refs[:count], refs[count : 2 * count], refs[2 * count : 3 * count], refs[-1]
    into, out = [], []
    for i in range(count):
        rows = ins[i].shape[0] // parts[i]
        for c in range(parts[i]):
            span = pl.ds(c * rows, rows)
            at = len(into)
            into.append(pltpu.make_async_copy(ins[i].at[span], held[i].at[span], sems.at[0, at]))
            out.append(pltpu.make_async_copy(held[i].at[span], outs[i].at[span], sems.at[1, at]))
    for copy in into:
        copy.start()
    for a, b in zip(into, out):
        a.wait()
        b.start()
    for copy in out:
        copy.wait()


def leave(*arrays):
    count = len(arrays)
    parts = [8 if a.ndim == 3 else 1 for a in arrays]
    hbm = pl.BlockSpec(memory_space=pl.ANY)
    return pl.pallas_call(
        functools.partial(leave_kernel, count, parts),
        out_shape=tuple(jax.ShapeDtypeStruct(a.shape, a.dtype) for a in arrays),
        in_specs=[hbm] * count,
        out_specs=(hbm,) * count,
        scratch_shapes=[pltpu.VMEM(a.shape, a.dtype) for a in arrays]
        + [pltpu.SemaphoreType.DMA((2, sum(parts)))],
        name="leave",
    )(*arrays)


def serve(n, tps, table, lens, queries, source, wanted, sizes, holder, slot, resident, swap, down, up):
    reqs, width = queries.shape
    pool, page, kvw = resident.shape
    news = source.size // n
    rows = n * 8
    smem = pl.BlockSpec(memory_space=pltpu.SMEM)
    vmem = pl.BlockSpec(memory_space=pltpu.VMEM)
    hbm = pl.BlockSpec(memory_space=pl.ANY)
    dma = pltpu.SemaphoreType.DMA
    bf16, f32 = jnp.bfloat16, jnp.float32
    stores = swap.shape[0]

    def held(count):
        return pltpu.VMEM((count, page, kvw), bf16)

    return pl.pallas_call(
        functools.partial(main_kernel, n, tps),
        out_shape=(
            jax.ShapeDtypeStruct((reqs, width), bf16),
            jax.ShapeDtypeStruct((reqs, width), bf16),
            jax.ShapeDtypeStruct((news, page, kvw), bf16),
        ),
        in_specs=[smem] * 2 + [hbm] * 10,
        out_specs=(hbm, vmem, hbm),
        scratch_shapes=[
            pltpu.VMEM(queries.shape, bf16),
            pltpu.VMEM(source.shape, jnp.int32),
            pltpu.VMEM(wanted.shape, jnp.int32),
            pltpu.VMEM(sizes.shape, jnp.int32),
            pltpu.VMEM(holder.shape, jnp.int32),
            pltpu.VMEM(slot.shape, jnp.int32),
            pltpu.VMEM(queries.shape, bf16),
            pltpu.VMEM((n, 64, LANES), bf16),
            held(pool + n * CAP),
            held(stores), held(stores), held(stores), held(stores), held(stores),
            held(NEAR), held(NEAR), held(NEAR - CHUNK), held(NEAR - CHUNK), held(CHUNK), held(CHUNK),
            held(NEAR), held(NEAR), held(2 * FAR),
            pltpu.VMEM((RZ, RX - 1, CAP, page, kvw), bf16),
            held(news),
            pltpu.VMEM((reqs * 8, LANES), f32),
            pltpu.VMEM((reqs * 8, LANES), f32),
            pltpu.VMEM(down.shape, bf16),
            pltpu.VMEM(up.shape, bf16),
            pltpu.VMEM((n, 64, LANES), bf16),
            pltpu.VMEM((n, 64, LANES), bf16),
            pltpu.VMEM((n, 64, LANES), bf16),
            pltpu.VMEM((GROUPS, rows // (2 * GROUPS), LANES), f32),
            pltpu.VMEM((GROUPS, tps - 1, rows // (2 * GROUPS), LANES), f32),
            pltpu.VMEM((16 + stores, LANES), jnp.int32),
            pltpu.SMEM((16 + stores, LANES), jnp.int32),
            dma((10,)),
            dma((2, stores // CHUNK)), dma((2, stores // CHUNK)),
            dma((2, stores // CHUNK)), dma((2, stores // CHUNK)),
            dma((2, NEAR // CHUNK)), dma((2, NEAR // CHUNK)), dma((2,)), dma((2,)),
            dma((RZ, RX - 1)), dma((RZ, RX - 1)),
            dma((n,)), dma((n,)), dma((n,)), dma((n,)),
            dma((GROUPS, tps - 1)), dma((GROUPS, tps - 1)),
        ],
        compiler_params=pltpu.CompilerParams(
            collective_id=0, has_side_effects=True, vmem_limit_bytes=56 << 20
        ),
        name="serve",
    )(table, lens, queries, source, wanted, sizes, holder, slot, resident, swap, down, up)


def local(
    queries,
    resident_kv,
    swap_kv,
    page_table,
    lengths,
    resume_source,
    resume_page,
    seg_lengths,
    segment_adapter_holder,
    seg_slot,
    adapter_down,
    adapter_up,
):
    results = serve(
        lax.axis_size("req"),
        lax.axis_size("tp"),
        page_table.T,
        lengths,
        queries,
        resume_source.reshape(-1, LANES),
        resume_page.reshape(-1, LANES),
        seg_lengths,
        segment_adapter_holder.reshape(-1, LANES),
        seg_slot.reshape(-1, LANES),
        resident_kv,
        swap_kv,
        adapter_down,
        adapter_up,
    )
    mixed, delta, arrived = results
    return leave(mixed, delta, arrived)


def solution(mesh):
    return jax.shard_map(
        local,
        mesh=mesh,
        in_specs=(
            P("req", "tp"),
            P("req", None, "tp"),
            P("req", None, "tp"),
            P("req", None),
            P("req"),
            P(),
            P(),
            P("req", None),
            P(),
            P(),
            P("req", None, "tp"),
            P("req", None, "tp"),
        ),
        out_specs=(P("req", "tp"), P("req", "tp"), P("req", None, "tp")),
        check_vma=False,
    )
```

```python
import functools

import jax
import jax.numpy as jnp
from jax import lax
from jax.experimental import pallas as pl
from jax.experimental.pallas import tpu as pltpu
from jax.sharding import PartitionSpec as P

HD = 128
SEGMAX = 4
LANES = 128
MESH = pl.DeviceIdType.MESH
NEG = -1e30
RZ, RX = 8, 4
CAP = 4
CHUNK = 8
NEAR = 24
FAR = 8
GROUPS = 4

low_rank_scale = 2.0


def iota(shape, dim):
    return lax.broadcasted_iota(jnp.int32, shape, dim)


def ones(mask):
    return jnp.where(mask, 1.0, 0.0)


def mm(a, b):
    return jnp.dot(
        a.astype(jnp.bfloat16), b.astype(jnp.bfloat16), preferred_element_type=jnp.float32
    )


def mmt(a, b):
    return lax.dot_general(
        a.astype(jnp.bfloat16),
        b.astype(jnp.bfloat16),
        (((1,), (1,)), ((), ())),
        preferred_element_type=jnp.float32,
    )


def before(n, block):
    r, c = iota((n, n), 0), iota((n, n), 1)
    return ones((r < c) & (r // block == c // block))


def row_of(x, i):
    return jnp.sum(jnp.where(iota(x.shape, 0) == i, x, jnp.zeros((), x.dtype)), axis=0, keepdims=True)


def ring_plan(source, wanted, zi, xi, stores, pages, per_block):
    shape = (RZ, pages)
    zs = iota(shape, 0)
    need, need_even = [], []
    for zd in range(RZ):
        total = jnp.zeros(shape, jnp.float32)
        even = jnp.zeros(shape, jnp.float32)
        for h in range(2):
            s = source[2 * zd + h : 2 * zd + h + 1]
            w = wanted[2 * zd + h : 2 * zd + h + 1]
            a = ones(iota((RZ, LANES), 0) * RX + xi == s)
            b = ones(iota((pages, LANES), 0) == w)
            total = total + mmt(a, b)
            x = 2 * h + iota((RZ, LANES), 1) // per_block
            even = even + mmt(a * ones(lax.rem(x - xi + RX, 2) == 0), b)
        need.append(total)
        need_even.append(even)

    def wants(needed, k):
        found = jnp.zeros(shape, jnp.float32)
        for zd in range(RZ):
            found = jnp.where(lax.rem(zd - zs + RZ, RZ) == k, needed[zd], found)
        return ones(found > 0.5)

    at = {k: wants(need, k) for k in (3, 4, 5)}
    at_even = {k: wants(need_even, k) for k in (3, 5)}
    tri = before(pages, pages)
    far = at[4]
    far_up = far * ones(mm(far, tri) < FAR - 0.5)
    far_down = far - far_up
    lists = {}
    for name, f4, k in (("up", far_up, 3), ("down", far_down, 5)):
        f3 = at[k] * (1.0 - f4)
        half = at_even[k] * f3
        other = f3 - half
        place4 = mm(f4, tri)
        place3 = half * (FAR + mm(half, tri)) + other * (NEAR - CHUNK + mm(other, tri))
        lists[name] = (f4, f3, place4, f4 * place4 + place3)
    page_id = iota(shape, 1).astype(jnp.float32)
    k = lax.rem(zi - zs + RZ, RZ)
    spot4 = jnp.where(far_up > 0.5, lists["up"][2], FAR + lists["down"][2])
    spot = jnp.where(
        k == 3, lists["up"][3], jnp.where(k == 5, lists["down"][3], jnp.where(k == 4, spot4, page_id))
    )
    send = []
    for name, owner in (("up", lax.rem(zi + RZ - 2, RZ)), ("down", lax.rem(zi + 2, RZ))):
        f4, f3, _, place = lists[name]
        used = row_of(f4 + f3, owner)
        p = row_of(place, owner)
        hit = (iota((pages, pages), 0).astype(jnp.float32) == p) & (used > 0.5)
        send.append(
            jnp.sum(
                jnp.where(hit, iota((pages, pages), 1).astype(jnp.float32), 0.0), axis=1, keepdims=True
            )
        )
    tri2 = before(LANES, per_block)
    table = jnp.zeros((RZ, LANES), jnp.float32)
    landing = []
    lane = iota((1, LANES), 1)
    for h in range(2):
        s = row_of(source, 2 * zi + h)
        w = row_of(wanted, 2 * zi + h)
        hot = ones(iota((stores, LANES), 0) == s)
        rank = jnp.sum(hot * mm(hot, tri2), axis=0, keepdims=True)
        landing.append(s.astype(jnp.float32) * CAP + rank)
        v = mm(spot, ones(iota((pages, LANES), 0) == w))
        v = v * ones(iota((RZ, LANES), 0) * RX + xi == s)
        column = (2 * h + lane // per_block) * CAP + rank.astype(jnp.int32)
        table = table + mmt(v, ones(iota((LANES, LANES), 0) == column))
    top = jnp.concatenate(
        [table, landing[0], landing[1], jnp.zeros((RZ - 2, LANES), jnp.float32)], axis=0
    )
    wide = iota((pages, LANES), 1)
    tail = jnp.where(wide == 0, send[0], jnp.where(wide == 1, send[1], 0.0))
    return jnp.concatenate([top, tail], axis=0).astype(jnp.int32)


def apart(p, n):
    return GROUPS * lax.rem(p, n // GROUPS) + p // (n // GROUPS)


def chain_plan(n, reqs, sizes, holder, slot, me):
    segs = sizes.shape[1]
    rows = n * 8
    blocks = LANES // segs
    tri = before(LANES, segs)
    mine = ones(holder == me)
    order = mm(mine, tri)

    def sender(number):
        return lax.rem(me - apart(number // 8, n) + n, n)

    wide = (rows, holder.shape[0])
    spread = sender(iota(wide, 0)) // blocks == iota(wide, 1)
    y = []
    for q in range(2):
        x = jnp.where((mine > 0.5) & (jnp.abs(order - q) < 0.5), slot, 0).astype(jnp.float32)
        y.append(mm(ones(spread), x))
    number = iota((rows, LANES), 0)
    pick = jnp.where(lax.rem(number // 4, 2) == 0, y[0], y[1])
    pick = jnp.where(iota((rows, LANES), 1) // segs == lax.rem(sender(number), blocks), pick, 0.0)
    held = jnp.sum(pick, axis=1, keepdims=True).astype(jnp.int32)

    own = row_of(holder, me // blocks)
    hot = ones(iota((n, LANES), 0) == own)
    rank = jnp.sum(hot * mm(hot, tri), axis=0, keepdims=True)
    away = lax.rem(own - me + n, n)
    block = lax.rem(away, GROUPS) * (n // GROUPS) + away // GROUPS
    value = (block.astype(jnp.float32) * 2 + rank) * SEGMAX
    diag = iota((segs, LANES), 1) == lax.rem(me, blocks) * segs + iota((segs, LANES), 0)
    value = jnp.sum(jnp.where(diag, value, 0.0), axis=1, keepdims=True)
    size = sizes.astype(jnp.float32)
    square = iota((segs, segs), 1) == iota((segs, segs), 0)
    wide = jnp.where(square, size, 0.0)
    size = jnp.sum(wide, axis=1, keepdims=True)
    start = jnp.sum(
        jnp.where(
            iota((segs, segs), 1) < iota((segs, segs), 0), sizes.astype(jnp.float32), 0.0
        ),
        axis=1,
        keepdims=True,
    )
    r = iota((segs, reqs), 1).astype(jnp.float32)
    inside = (r >= start) & (r < start + size)
    place = jnp.sum(jnp.where(inside, value - start + r, 0.0), axis=0, keepdims=True)
    return place.astype(jnp.int32), held


def by_heads(x, rows, heads):
    return jnp.concatenate(
        [x[:, h * 8 : (h + 1) * 8, :].reshape(rows, LANES) for h in range(heads)], axis=1
    )


def main_kernel(
    n, tps,
    table_in, lens_in, q_in, source_in, wanted_in, sizes_in, holder_in, slot_in,
    resident, swap, down_in, up_in,
    mixed, delta_ref, arrived,
    table, lens, q_ref, source, wanted, sizes, holder, slot, out_ref, ret,
    space, store, near_up, near_down, next_up, next_down, on_up, on_down, third_up, third_down,
    rest_up, rest_down, all_up, all_down,
    fourth, crossing, arr, qs, att, down, up, send, got, back, part, parts, plan, book,
    load, s1, r1, s2, r2, s3, r3, s4, r4, sx, rx, ss, rs, sb, rb, st, rt,
):
    reqs, width = q_ref.shape
    heads = width // HD
    pool, page = resident.shape[0], resident.shape[1]
    maxp = table.shape[0]
    news = arr.shape[0]
    pages = store.shape[0]
    slots, rank = down.shape[0], down.shape[1]
    rows = n * 8
    me, tp = lax.axis_index("req"), lax.axis_index("tp")
    zi, xi = me // RX, lax.rem(me, RX)
    above = lax.rem(zi + 1, RZ) * RX + xi
    below = lax.rem(zi + RZ - 1, RZ) * RX + xi
    barrier = pltpu.get_barrier_semaphore()

    loads = [
        pltpu.make_async_copy(swap, store, load.at[0]),
        pltpu.make_async_copy(resident, space.at[pl.ds(0, pool)], load.at[1]),
        pltpu.make_async_copy(down_in, down, load.at[2]),
        pltpu.make_async_copy(up_in, up, load.at[3]),
    ]
    small = [
        pltpu.make_async_copy(a, b, load.at[4 + i])
        for i, (a, b) in enumerate(
            (
                (source_in, source),
                (wanted_in, wanted),
                (sizes_in, sizes),
                (holder_in, holder),
                (slot_in, slot),
                (q_in, q_ref),
                (table_in, table),
                (lens_in, lens),
            )
        )
    ]
    loads[0].start()
    for copy in small:
        copy.start()

    def hello(d, c):
        pl.semaphore_signal(
            barrier, inc=1, device_id={"req": lax.rem(me + d, n)}, device_id_type=MESH
        )
        return c

    lax.fori_loop(1, n, hello, 0)
    for d in range(1, tps):
        pl.semaphore_signal(
            barrier, inc=1, device_id={"tp": lax.rem(tp + d, tps)}, device_id_type=MESH
        )
    loads[0].wait()
    pl.semaphore_wait(barrier, n - 1 + tps - 1)

    def hop(src, dst, ssem, rsem, to):
        return pltpu.make_async_remote_copy(
            src_ref=src, dst_ref=dst, send_sem=ssem, recv_sem=rsem,
            device_id={"req": to}, device_id_type=MESH,
        )

    sides = (above, below)
    near, nxt, on, third = (
        (near_up, near_down), (next_up, next_down), (on_up, on_down), (third_up, third_down)
    )
    rest, whole = (rest_up, rest_down), (all_up, all_down)
    early = NEAR // CHUNK - 1

    def part_of(ref, c):
        return ref.at[pl.ds(c * CHUNK, CHUNK)]

    first, second, later, last = [], [], [], []
    for c in range(pages // CHUNK):
        for w in range(2):
            first.append(
                hop(part_of(store, c), part_of(near[w], c), s1.at[w, c], r1.at[w, c], sides[w])
            )
            second.append(
                hop(part_of(near[w], c), part_of(nxt[w], c), s2.at[w, c], r2.at[w, c], sides[w])
            )
    for c in range(NEAR // CHUNK):
        for w in range(2):
            to = part_of(third[w], c) if c < early else rest[w]
            later.append(hop(part_of(on[w], c), to, s3.at[w, c], r3.at[w, c], sides[w]))
    for w in range(2):
        last.append(
            hop(third[w].at[pl.ds(0, FAR)], part_of(fourth, w), s4.at[w], r4.at[w], sides[w])
        )
    for copy in first:
        copy.start()
    for copy in loads[1:]:
        copy.start()

    for copy in small:
        copy.wait()
    plan[...] = ring_plan(source[...], wanted[...], zi, xi, n, pages, news)
    enter = pltpu.make_async_copy(plan, book, load.at[0])
    enter.start()
    slot_place, hs = chain_plan(n, reqs, sizes[...], holder[...], slot[...], me)
    put = ones(iota((rows, reqs), 0) == slot_place).astype(jnp.bfloat16)
    qs[...] = jnp.zeros_like(qs)
    for h in range(heads):
        qs[pl.ds(h, reqs, stride=8), :] = q_ref[:, h * HD : (h + 1) * HD].astype(jnp.float32)
    enter.wait()

    def within(i, ref):
        return jnp.clip(i, 0, ref.shape[0] - 1)

    def land(z, x):
        return pool + (z * RX + x) * CAP

    def cross_copy(k, dx):
        z = lax.rem(zi + RZ - k, RZ)
        return hop(
            crossing.at[k, dx - 1], space.at[pl.ds(land(z, xi), CAP)],
            sx.at[k, dx - 1], rx.at[k, dx - 1], z_row(dx),
        )

    def z_row(dx):
        return zi * RX + lax.rem(xi + dx, RX)

    def cross(k, ref, ways=(2, 1, 3, 0)):
        z = lax.rem(zi + RZ - k, RZ)
        for dx in ways:
            if dx == 0:
                for r in range(CAP):
                    space[land(z, xi) + r] = ref[within(book[z, xi * CAP + r], ref)]
                continue
            xd = lax.rem(xi + dx, RX)
            for r in range(CAP):
                crossing[k, dx - 1, r] = ref[within(book[z, xd * CAP + r], ref)]
            cross_copy(k, dx).start()

    cross(0, store)
    for a, b in zip(first, second):
        a.wait_recv()
        b.start()
    cross(1, near_up)
    cross(7, near_down)
    for copy in second:
        copy.wait_recv()
    for c in range(NEAR // CHUNK):
        for w in range(2):
            for i in range(CHUNK):
                on[w][c * CHUNK + i] = nxt[w][within(book[16 + c * CHUNK + i, w], nxt[w])]
            later[c * 2 + w].start()
    cross(2, next_up)
    cross(6, next_down)
    for i, copy in enumerate(later[: 2 * early]):
        copy.wait_recv()
        if i < 2:
            last[i].start()
    cross(3, third_up, (2, 0))
    cross(5, third_down, (2, 0))
    for w in range(2):
        whole[w][pl.ds(0, early * CHUNK)] = third[w][...]
    for copy in later[2 * early :]:
        copy.wait_recv()
    for w in range(2):
        whole[w][pl.ds(early * CHUNK, CHUNK)] = rest[w][...]
    cross(3, all_up, (1, 3))
    cross(5, all_down, (1, 3))
    for copy in last:
        copy.wait_recv()
    cross(4, fourth)
    for copy in loads[1:]:
        copy.wait()
    for k in range(RZ):
        for dx in range(1, RX):
            z = lax.rem(zi + RZ - k, RZ)
            x = lax.rem(xi + RX - dx, RX)
            hop(
                crossing.at[k, dx - 1], space.at[pl.ds(land(z, x), CAP)],
                sx.at[k, dx - 1], rx.at[k, dx - 1], z_row(dx),
            ).wait_recv()

    def spot(j):
        return pool + jnp.clip(book[8 + xi // 2, lax.rem(xi, 2) * news + j], 0, n * CAP - 1)

    step = 32

    def page_at(r, k):
        t = table[k, r]
        return jnp.where(t < pool, jnp.clip(t, 0, pool - 1), spot(jnp.clip(t - pool, 0, news - 1)))

    def body(b, c):
        scores, spots = [], []
        for i in range(step):
            r = b * step + i
            at = [page_at(r, k) for k in range(maxp)]
            keys = jnp.concatenate([space[a, :, :HD] for a in at], axis=0)
            q = qs[pl.ds(pl.multiple_of(r * 8, 8), 8), :].astype(jnp.bfloat16)
            s = lax.dot_general(
                q, keys, (((1,), (1,)), ((), ())), preferred_element_type=jnp.float32
            ) * (HD ** (-0.5))
            pos = lax.broadcasted_iota(jnp.int32, s.shape, 1)
            scores.append(jnp.where(pos < lens[r], s, NEG))
            spots.append(at)
        s = jnp.concatenate(scores, axis=0)
        e = jnp.exp(s - jnp.max(s, axis=1, keepdims=True))
        p = e / jnp.sum(e, axis=1, keepdims=True)
        for i in range(step):
            vals = jnp.concatenate([space[a, :, HD:] for a in spots[i]], axis=0)
            o = jnp.dot(
                p[i * 8 : (i + 1) * 8].astype(jnp.bfloat16),
                vals,
                preferred_element_type=jnp.float32,
            )
            att[pl.ds(pl.multiple_of((b * step + i) * 8, 8), 8), :] = o
        return c

    lax.fori_loop(0, reqs // step, body, 0)
    for h in range(heads):
        out_ref[:, h * HD : (h + 1) * HD] = att[pl.ds(h, reqs, stride=8), :].astype(jnp.bfloat16)

    keep_mixed = pltpu.make_async_copy(out_ref, mixed, load.at[1])
    keep_mixed.start()
    g = jnp.dot(put, out_ref[...], preferred_element_type=jnp.float32)
    zero = jnp.zeros((8, LANES), jnp.float32)
    groups = GROUPS
    blocks = n // groups
    group_rows = blocks * 8

    def there(p):
        to = lax.rem(me + apart(p, n), n)
        return hop(send.at[p], got.at[p], ss.at[p], rs.at[p], to)

    def home(p):
        to = lax.rem(me - apart(p, n) + n, n)
        return hop(ret.at[p], back.at[p], sb.at[p], rb.at[p], to)

    def each(group, act):
        def one(p, c):
            act(p)
            return c

        lax.fori_loop(max(1, group * blocks), (group + 1) * blocks, one, 0)

    for group in range(groups):
        for p in range(group * blocks, (group + 1) * blocks):
            block = [g[p * 8 : (p + 1) * 8, h * HD : (h + 1) * HD] for h in range(heads)]
            block += [zero] * (8 - heads)
            send[p] = jnp.concatenate(block, axis=0).astype(jnp.bfloat16)
        each(group, lambda p: there(p).start())
    got[0] = send[0]

    lane = iota((group_rows, LANES), 1)
    per = LANES // rank
    half = group_rows // 2
    low = iota((half, LANES), 1) < rank
    exchange = []
    for group in range(groups):
        exchange.append(
            [
                pltpu.make_async_remote_copy(
                    src_ref=part.at[group], dst_ref=parts.at[group, d - 1],
                    send_sem=st.at[group, d - 1], recv_sem=rt.at[group, d - 1],
                    device_id={"tp": lax.rem(tp + d, tps)}, device_id_type=MESH,
                )
                for d in range(1, tps)
            ]
        )
    held = [hs[group * group_rows : (group + 1) * group_rows] for group in range(groups)]

    def shrink(group):
        each(group, lambda p: there(p).wait_recv())
        mine = slice(group * blocks, (group + 1) * blocks)
        a = by_heads(got[mine].astype(jnp.float32), group_rows, heads).astype(jnp.bfloat16)
        total = jnp.zeros((group_rows, LANES), jnp.float32)
        for c in range(0, slots, 2 * per):
            w = down[c : c + 2 * per].reshape(2 * per * rank, width)
            s = mmt(a, w)
            total = total + jnp.where(held[group] == c + lane // rank, s[:, :LANES], 0.0)
            total = total + jnp.where(held[group] == c + per + lane // rank, s[:, LANES:], 0.0)
        total = total + pltpu.roll(total, rank, 1)
        part[group] = jnp.where(low, total[:half], total[half:])
        for copy in exchange[group]:
            copy.start()

    def expand(group):
        for copy in exchange[group]:
            copy.wait_recv()
        acc = part[group]
        for d in range(tps - 1):
            acc = acc + parts[group, d]
        turned = pltpu.roll(acc, rank, 1)
        shrunk = jnp.concatenate(
            [jnp.where(low, acc, turned), jnp.where(low, turned, acc)], axis=0
        ).astype(jnp.bfloat16)
        spread = jnp.concatenate(
            [
                jnp.where(held[group] == c + lane // rank, shrunk, jnp.zeros((), jnp.bfloat16))
                for c in range(0, slots, per)
            ],
            axis=1,
        )
        t = mm(spread, up[...].reshape(slots * rank, width)) * low_rank_scale
        for p in range(blocks):
            block = [t[p * 8 : (p + 1) * 8, h * HD : (h + 1) * HD] for h in range(heads)]
            block += [zero] * (8 - heads)
            ret[group * blocks + p] = jnp.concatenate(block, axis=0).astype(jnp.bfloat16)
        each(group, lambda p: home(p).start())

    def pick(j, c):
        arr[j] = space[spot(j)]
        return c

    lax.fori_loop(0, news, pick, 0)
    keep = pltpu.make_async_copy(arr, arrived, load.at[0])
    keep.start()
    shrink(0)
    shrink(1)
    expand(0)
    shrink(2)
    expand(1)
    shrink(3)
    expand(2)
    expand(3)
    back[0] = ret[0]
    for group in range(groups):
        each(group, lambda p: there(p).wait_send())
        for copy in exchange[group]:
            copy.wait_send()
    for copy in first + second + later + last:
        copy.wait_send()
    for k in range(RZ):
        for dx in range(1, RX):
            cross_copy(k, dx).wait_send()
    keep.wait()
    keep_mixed.wait()
    for group in range(groups):
        each(group, lambda p: home(p).wait_recv())
    b = by_heads(back[...].astype(jnp.float32), rows, heads).astype(jnp.bfloat16)
    delta_ref[...] = lax.dot_general(
        put, b, (((0,), (0,)), ((), ())), preferred_element_type=jnp.float32
    ).astype(jnp.bfloat16)
    for group in range(groups):
        each(group, lambda p: home(p).wait_send())


def leave_kernel(count, parts, *refs):
    ins, outs, held, sems = refs[:count], refs[count : 2 * count], refs[2 * count : 3 * count], refs[-1]
    into, out = [], []
    for i in range(count):
        rows = ins[i].shape[0] // parts[i]
        for c in range(parts[i]):
            span = pl.ds(c * rows, rows)
            at = len(into)
            into.append(pltpu.make_async_copy(ins[i].at[span], held[i].at[span], sems.at[0, at]))
            out.append(pltpu.make_async_copy(held[i].at[span], outs[i].at[span], sems.at[1, at]))
    for copy in into:
        copy.start()
    for a, b in zip(into, out):
        a.wait()
        b.start()
    for copy in out:
        copy.wait()


def leave(*arrays):
    count = len(arrays)
    parts = [8 if a.ndim == 3 else 1 for a in arrays]
    hbm = pl.BlockSpec(memory_space=pl.ANY)
    return pl.pallas_call(
        functools.partial(leave_kernel, count, parts),
        out_shape=tuple(jax.ShapeDtypeStruct(a.shape, a.dtype) for a in arrays),
        in_specs=[hbm] * count,
        out_specs=(hbm,) * count,
        scratch_shapes=[pltpu.VMEM(a.shape, a.dtype) for a in arrays]
        + [pltpu.SemaphoreType.DMA((2, sum(parts)))],
        name="leave",
    )(*arrays)


def serve(n, tps, table, lens, queries, source, wanted, sizes, holder, slot, resident, swap, down, up):
    reqs, width = queries.shape
    pool, page, kvw = resident.shape
    news = source.size // n
    rows = n * 8
    vmem = pl.BlockSpec(memory_space=pltpu.VMEM)
    hbm = pl.BlockSpec(memory_space=pl.ANY)
    dma = pltpu.SemaphoreType.DMA
    bf16, f32 = jnp.bfloat16, jnp.float32
    stores = swap.shape[0]

    def held(count):
        return pltpu.VMEM((count, page, kvw), bf16)

    return pl.pallas_call(
        functools.partial(main_kernel, n, tps),
        out_shape=(
            jax.ShapeDtypeStruct((reqs, width), bf16),
            jax.ShapeDtypeStruct((reqs, width), bf16),
            jax.ShapeDtypeStruct((news, page, kvw), bf16),
        ),
        in_specs=[hbm] * 12,
        out_specs=(hbm, vmem, hbm),
        scratch_shapes=[
            pltpu.SMEM(table.shape, jnp.int32),
            pltpu.SMEM(lens.shape, jnp.int32),
            pltpu.VMEM(queries.shape, bf16),
            pltpu.VMEM(source.shape, jnp.int32),
            pltpu.VMEM(wanted.shape, jnp.int32),
            pltpu.VMEM(sizes.shape, jnp.int32),
            pltpu.VMEM(holder.shape, jnp.int32),
            pltpu.VMEM(slot.shape, jnp.int32),
            pltpu.VMEM(queries.shape, bf16),
            pltpu.VMEM((n, 64, LANES), bf16),
            held(pool + n * CAP),
            held(stores), held(stores), held(stores), held(stores), held(stores),
            held(NEAR), held(NEAR), held(NEAR - CHUNK), held(NEAR - CHUNK), held(CHUNK), held(CHUNK),
            held(NEAR), held(NEAR), held(2 * FAR),
            pltpu.VMEM((RZ, RX - 1, CAP, page, kvw), bf16),
            held(news),
            pltpu.VMEM((reqs * 8, LANES), f32),
            pltpu.VMEM((reqs * 8, LANES), f32),
            pltpu.VMEM(down.shape, bf16),
            pltpu.VMEM(up.shape, bf16),
            pltpu.VMEM((n, 64, LANES), bf16),
            pltpu.VMEM((n, 64, LANES), bf16),
            pltpu.VMEM((n, 64, LANES), bf16),
            pltpu.VMEM((GROUPS, rows // (2 * GROUPS), LANES), f32),
            pltpu.VMEM((GROUPS, tps - 1, rows // (2 * GROUPS), LANES), f32),
            pltpu.VMEM((16 + stores, LANES), jnp.int32),
            pltpu.SMEM((16 + stores, LANES), jnp.int32),
            dma((12,)),
            dma((2, stores // CHUNK)), dma((2, stores // CHUNK)),
            dma((2, stores // CHUNK)), dma((2, stores // CHUNK)),
            dma((2, NEAR // CHUNK)), dma((2, NEAR // CHUNK)), dma((2,)), dma((2,)),
            dma((RZ, RX - 1)), dma((RZ, RX - 1)),
            dma((n,)), dma((n,)), dma((n,)), dma((n,)),
            dma((GROUPS, tps - 1)), dma((GROUPS, tps - 1)),
        ],
        compiler_params=pltpu.CompilerParams(
            collective_id=0, has_side_effects=True, vmem_limit_bytes=56 << 20
        ),
        name="serve",
    )(table, lens, queries, source, wanted, sizes, holder, slot, resident, swap, down, up)


def local(
    queries,
    resident_kv,
    swap_kv,
    page_table,
    lengths,
    resume_source,
    resume_page,
    seg_lengths,
    segment_adapter_holder,
    seg_slot,
    adapter_down,
    adapter_up,
):
    results = serve(
        lax.axis_size("req"),
        lax.axis_size("tp"),
        page_table.T,
        lengths,
        queries,
        resume_source.reshape(-1, LANES),
        resume_page.reshape(-1, LANES),
        seg_lengths,
        segment_adapter_holder.reshape(-1, LANES),
        seg_slot.reshape(-1, LANES),
        resident_kv,
        swap_kv,
        adapter_down,
        adapter_up,
    )
    mixed, delta, arrived = results
    return leave(mixed, delta, arrived)


def solution(mesh):
    return jax.shard_map(
        local,
        mesh=mesh,
        in_specs=(
            P("req", "tp"),
            P("req", None, "tp"),
            P("req", None, "tp"),
            P("req", None),
            P("req"),
            P(),
            P(),
            P("req", None),
            P(),
            P(),
            P("req", None, "tp"),
            P("req", None, "tp"),
        ),
        out_specs=(P("req", "tp"), P("req", "tp"), P("req", None, "tp")),
        check_vma=False,
    )
```
